32 devices in a mesh: crop: 1, res: 32 (over z, y, x, core).
Axes of the slice: x: 2, y: 2, z: 4, core: 2. Of those that a mesh axis runs over, the one named last changes fastest.
Arguments:
- homolog_symbol_ids: int32 [64, 128], P(('crop', 'res')), may hold values from 0 to 22
- residue_attend_mask: int32 [128], P('crop'), may hold values 0 or 1
- alignment_state: bfloat16 [64, 128, 256], P(('crop', 'res')), may hold values from -6 to 6
- pair: bfloat16 [128, 128, 128], P(('crop', 'res')), may hold values from -6 to 6
- symbol_lookup_matrix: bfloat16 [23, 256], replicated, may hold values from -3 to 3
- pair_bias_weight: bfloat16 [128, 8], replicated, may hold values from -0.5 to 0.5
- row_projection_weight: bfloat16 [256, 1024], replicated, may hold values from -8 to 8
- horizontal_readout_matrix: bfloat16 [256, 256], replicated, may hold values from -0.375 to 0.375
- column_projection_weight: bfloat16 [256, 1024], replicated, may hold values from -8 to 8
- vertical_readout_matrix: bfloat16 [256, 256], replicated, may hold values from -0.375 to 0.375
- product_factor_matrices: bfloat16 [256, 64], replicated, may hold values from -0.375 to 0.375
- outer_output_weight: bfloat16 [1024, 128], replicated, may hold values from -1.5 to 1.5
- triangle_input_weight: bfloat16 [128, 640], replicated, may hold values from -0.5 to 0.5
- triangle_output_weight: bfloat16 [128, 128], replicated, may hold values from -0.5 to 0.5
Outputs:
- alignment_output: bfloat16 [64, 128, 256], P('crop', 'res')
- pair_output: bfloat16 [128, 128, 128], P(('crop', 'res'))
The draws below stay inside these ranges and needn't reach their ends.
All inputs are finite; a program needn't handle non-finite values.
Results may differ from the reference program's by a relative error of at most 0.013.
Values may be sent and summed in bfloat16 or wider, within the bound.
No kernel may reach another device: no remote copies, remote signals or barrier semaphores. Data moves between devices by JAX's collectives and lax.ppermute only.
A program may use at most 64 MiB of HBM per device.

```python
import jax
import jax.numpy as jnp
from jax import lax

FEATURE_DEPTH = 256
CZ = 128
HEAD_NUMBER = 8
PRODUCT_WIDTH = 32
AMINO_VOCAB = 23
HOMOLOG_NUMBER = 64
CHAIN_LENGTH = 128


def draw_alignment_state(key, part):
    random_seed_primary = jax.random.fold_in(jax.random.fold_in(key, 3), 0)
    lower_bound_index = jax.random.normal(random_seed_primary, (HOMOLOG_NUMBER, CHAIN_LENGTH, FEATURE_DEPTH), jnp.float32)
    return jnp.clip(lower_bound_index, -6.0, 6.0).astype(jnp.bfloat16)


def draw_projection(key, channels):
    weight = jnp.clip(jax.random.normal(key, (channels, 4 * channels), jnp.float32), -4.0, 4.0) * channels ** (-0.5)
    return weight.astype(jnp.bfloat16)


def draw_row_projection_weight(key, part):
    return draw_projection(jax.random.fold_in(key, 11), FEATURE_DEPTH)


def draw_column_projection_weight(key, part):
    return draw_projection(jax.random.fold_in(key, 29), FEATURE_DEPTH)


def touch_ends(result, key, smallest, high):
    extent = result.shape
    place = [jax.random.randint(jax.random.fold_in(key, axis), (), 0, extent[axis]) for axis in range(len(extent))]
    result = result.at[tuple(place)].set(smallest)
    longest = extent.index(max(extent))
    place[longest] = (place[longest] + 1) % extent[longest]
    return result.at[tuple(place)].set(high)


def shard_levels(key, shape, pieces, smallest, largest):
    factor_of, own = 1.0, jax.random.fold_in(key, 6)
    for position, blocks in pieces:
        heights = jnp.exp(jax.random.uniform(jax.random.fold_in(own, position), (blocks,), jnp.float32, smallest / len(pieces), largest / len(pieces)))
        factor_of = factor_of * jnp.repeat(heights, shape[position] // blocks).reshape([-1 if axis == position else 1 for axis in range(len(shape))])
    return factor_of


def bell_draw(key, extent, scale, reach, cuts=(), kind=jnp.bfloat16):
    loudness = shard_levels(key, extent, cuts, -0.22, 0.18) if cuts else 1.0
    entries = jax.random.normal(key, extent, jnp.float32) * scale * loudness
    return jnp.minimum(jnp.maximum(entries, -reach), reach).astype(kind)


def setup_inputs(seed: int = 0, part: int = 0) -> dict:
    seeds = jax.random.split(jax.random.key(seed), 15)
    part_keys = jax.random.split(jax.random.fold_in(seeds[14], part), 15)
    homolog_symbol_ids = touch_ends(jax.random.randint(part_keys[0], (HOMOLOG_NUMBER, CHAIN_LENGTH), 0, AMINO_VOCAB), jax.random.fold_in(part_keys[0], 1), 0, AMINO_VOCAB - 1).astype(jnp.int32)
    residue_attend_mask = touch_ends((jax.random.randint(part_keys[1], (CHAIN_LENGTH,), 0, 8) < 7).astype(jnp.int32), jax.random.fold_in(part_keys[1], 1), 0, 1)
    alignment_state = draw_alignment_state(jax.random.fold_in(jax.random.fold_in(seeds[14], part), 71), part)
    pair = bell_draw(part_keys[3], (CHAIN_LENGTH, CHAIN_LENGTH, CZ), 1.0, 6.0, ((0, 32),))
    symbol_lookup_matrix = bell_draw(seeds[4], (AMINO_VOCAB, FEATURE_DEPTH), 0.5, 3.0)
    pair_bias_weight = bell_draw(seeds[5], (CZ, HEAD_NUMBER), CZ ** -0.5, 0.5)
    row_projection_weight = draw_row_projection_weight(jax.random.fold_in(seeds[14], 71), part)
    horizontal_readout_matrix = bell_draw(seeds[7], (FEATURE_DEPTH, FEATURE_DEPTH), FEATURE_DEPTH ** -0.5, 0.375)
    column_projection_weight = draw_column_projection_weight(jax.random.fold_in(seeds[14], 71), part)
    vertical_readout_matrix = bell_draw(seeds[9], (FEATURE_DEPTH, FEATURE_DEPTH), FEATURE_DEPTH ** -0.5, 0.375)
    product_factor_matrices = bell_draw(seeds[10], (FEATURE_DEPTH, 2 * PRODUCT_WIDTH), FEATURE_DEPTH ** -0.5, 0.375)
    outer_output_weight = bell_draw(seeds[11], (PRODUCT_WIDTH * PRODUCT_WIDTH, CZ), (PRODUCT_WIDTH * PRODUCT_WIDTH // 64) ** -0.5, 1.5)
    triangle_input_weight = bell_draw(seeds[12], (CZ, 5 * CZ), CZ ** -0.5, 0.5)
    triangle_output_weight = bell_draw(seeds[13], (CZ, CZ), CZ ** -0.5, 0.5)
    return dict(homolog_symbol_ids=homolog_symbol_ids, residue_attend_mask=residue_attend_mask, alignment_state=alignment_state, pair=pair, symbol_lookup_matrix=symbol_lookup_matrix, pair_bias_weight=pair_bias_weight, row_projection_weight=row_projection_weight, horizontal_readout_matrix=horizontal_readout_matrix, column_projection_weight=column_projection_weight, vertical_readout_matrix=vertical_readout_matrix, product_factor_matrices=product_factor_matrices, outer_output_weight=outer_output_weight, triangle_input_weight=triangle_input_weight, triangle_output_weight=triangle_output_weight)


EPSILON = 1e-05

def layer_normalized(input_rows, axis):
    average = lax.optimization_barrier(jnp.mean(input_rows, axis, keepdims=True))
    centred = input_rows - average
    spread = lax.optimization_barrier(jnp.mean(centred * centred, axis, keepdims=True))
    return centred * lax.rsqrt(spread + EPSILON)

def split_proj(input_rows, weight):
    channels = weight.shape[0]
    head_size = channels // HEAD_NUMBER
    projected = jnp.dot(input_rows, weight, preferred_element_type=jnp.float32)
    query_tensor = (projected[:, :channels] * head_size ** (-0.5)).astype(jnp.bfloat16).reshape(-1, HEAD_NUMBER, head_size)
    key_tensor = projected[:, channels:2 * channels].astype(jnp.bfloat16).reshape(-1, HEAD_NUMBER, head_size)
    value_tensor = projected[:, 2 * channels:3 * channels].astype(jnp.bfloat16).reshape(-1, HEAD_NUMBER, head_size)
    gate_values = projected[:, 3 * channels:]
    return (query_tensor, key_tensor, value_tensor, gate_values)

def gated_attention(query_tensor, key_tensor, value_tensor, gate_values, extra_bias, out_weight):
    scores = jnp.einsum('qhd,khd->hqk', query_tensor.astype(jnp.float32), key_tensor.astype(jnp.float32)) + extra_bias
    row_top = lax.optimization_barrier(jnp.max(scores, -1, keepdims=True))
    exp_scores = jnp.exp(scores - row_top)
    weights = (exp_scores / lax.optimization_barrier(jnp.sum(exp_scores, -1, keepdims=True))).astype(jnp.bfloat16)
    mixed = jnp.einsum('hqk,khd->qhd', weights.astype(jnp.float32), value_tensor.astype(jnp.float32))
    gated = (jax.nn.sigmoid(gate_values) * mixed.reshape(gate_values.shape)).astype(jnp.bfloat16)
    return jnp.dot(gated, out_weight, preferred_element_type=jnp.float32)

def reference(homolog_symbol_ids, residue_attend_mask, alignment_state, pair, symbol_lookup_matrix, pair_bias_weight, row_projection_weight, horizontal_readout_matrix, column_projection_weight, vertical_readout_matrix, product_factor_matrices, outer_output_weight, triangle_input_weight, triangle_output_weight):
    one_hot_tokens = (homolog_symbol_ids[:, :, None] == jnp.arange(AMINO_VOCAB, dtype=jnp.int32)[None, None, :]).astype(jnp.float32)
    alignment_initial = alignment_state.astype(jnp.float32) + jnp.einsum('kly,yb->klb', one_hot_tokens, symbol_lookup_matrix.astype(jnp.float32))
    pair_normed = layer_normalized(pair.astype(jnp.float32), -1).astype(jnp.bfloat16)
    bias_full = jnp.einsum('ijc,ch->hij', pair_normed.astype(jnp.float32), pair_bias_weight.astype(jnp.float32)).astype(jnp.bfloat16)
    mask_bias = (residue_attend_mask.astype(jnp.float32) - 1.0) * 10000.0
    extra_bias = bias_full.astype(jnp.float32) + mask_bias[None, None, :]

    def row_update_one(alignment_row):
        input_rows = layer_normalized(alignment_row, -1).astype(jnp.bfloat16)
        query_tensor, key_tensor, value_tensor, gate_values = split_proj(input_rows, row_projection_weight)
        return (alignment_row + gated_attention(query_tensor, key_tensor, value_tensor, gate_values, extra_bias, horizontal_readout_matrix)).astype(jnp.bfloat16)
    alignment_after_rows = lax.map(row_update_one, alignment_initial)

    def column_update_one(column):
        column_start = column.astype(jnp.float32)
        input_rows = layer_normalized(column_start, -1).astype(jnp.bfloat16)
        query_tensor, key_tensor, value_tensor, gate_values = split_proj(input_rows, column_projection_weight)
        return column_start + gated_attention(query_tensor, key_tensor, value_tensor, gate_values, jnp.float32(0.0), vertical_readout_matrix)
    alignment_after_columns = lax.map(column_update_one, jnp.swapaxes(alignment_after_rows, 0, 1))
    alignment_output = jnp.swapaxes(alignment_after_columns, 0, 1).astype(jnp.bfloat16)
    outer_input = layer_normalized(alignment_after_columns, -1).astype(jnp.bfloat16)
    factor_ab = jnp.einsum('rsc,ce->rse', outer_input.astype(jnp.float32), product_factor_matrices.astype(jnp.float32))
    left = factor_ab[..., :PRODUCT_WIDTH].astype(jnp.bfloat16)
    latter_factor = factor_ab[..., PRODUCT_WIDTH:].astype(jnp.bfloat16)

    def opm_one(former_factor_vector):
        cross_product_result = (jnp.einsum('vf,avt->aft', former_factor_vector.astype(jnp.float32), latter_factor.astype(jnp.float32)) / HOMOLOG_NUMBER).astype(jnp.bfloat16)
        return jnp.dot(cross_product_result.reshape(CHAIN_LENGTH, PRODUCT_WIDTH * PRODUCT_WIDTH), outer_output_weight, preferred_element_type=jnp.float32)
    update = lax.map(opm_one, left)
    pair_one = pair.astype(jnp.float32) + update
    tri_normed = layer_normalized(pair_one, -1).astype(jnp.bfloat16)
    projected = jnp.einsum('ijc,ce->ije', tri_normed.astype(jnp.float32), triangle_input_weight.astype(jnp.float32))
    left_f = (jax.nn.sigmoid(projected[..., CZ:2 * CZ]) * projected[..., :CZ]).astype(jnp.bfloat16)
    right_f = (jax.nn.sigmoid(projected[..., 3 * CZ:4 * CZ]) * projected[..., 2 * CZ:3 * CZ]).astype(jnp.bfloat16)
    gate_out = projected[..., 4 * CZ:]
    combined = jnp.einsum('ikc,jkc->ijc', left_f.astype(jnp.float32), right_f.astype(jnp.float32)).astype(jnp.bfloat16)
    comb_normed = layer_normalized(combined.astype(jnp.float32), -1).astype(jnp.bfloat16)
    tri_update = jnp.dot(comb_normed, triangle_output_weight, preferred_element_type=jnp.float32)
    pair_output = (pair_one + jax.nn.sigmoid(gate_out) * tri_update).astype(jnp.bfloat16)
    return (alignment_output, pair_output)
```

```python
import jax
import jax.numpy as jnp
from jax import lax
from jax.sharding import PartitionSpec as P

EPSILON = 1e-05


def layer_normalized(input_rows, axis):
    average = jnp.mean(input_rows, axis, keepdims=True)
    centred = input_rows - average
    spread = jnp.mean(centred * centred, axis, keepdims=True)
    return centred * lax.rsqrt(spread + EPSILON)


def split_proj(input_rows, weight, head_count):
    channels = weight.shape[0]
    head_size = channels // head_count
    projected = jnp.einsum("blc,ce->ble", input_rows, weight, preferred_element_type=jnp.float32)
    lead = projected.shape[:2]
    query_tensor = (
        (projected[..., :channels] * head_size ** (-0.5))
        .astype(jnp.bfloat16)
        .reshape(lead + (head_count, head_size))
    )
    key_tensor = (
        projected[..., channels : 2 * channels]
        .astype(jnp.bfloat16)
        .reshape(lead + (head_count, head_size))
    )
    value_tensor = (
        projected[..., 2 * channels : 3 * channels]
        .astype(jnp.bfloat16)
        .reshape(lead + (head_count, head_size))
    )
    gate_values = projected[..., 3 * channels :]
    return (query_tensor, key_tensor, value_tensor, gate_values)


def attention_block_fn(query_tensor, key_tensor, value_tensor, gate_values, extra_bias, out_weight):
    scores = (
        jnp.einsum("bqhd,bkhd->bhqk", query_tensor, key_tensor, preferred_element_type=jnp.float32)
        + extra_bias
    )
    row_top = jnp.max(scores, -1, keepdims=True)
    exp_scores = jnp.exp(scores - row_top)
    weights = (exp_scores / jnp.sum(exp_scores, -1, keepdims=True)).astype(jnp.bfloat16)
    mixed = jnp.einsum("bhqk,bkhd->bqhd", weights, value_tensor, preferred_element_type=jnp.float32)
    gated = (jax.nn.sigmoid(gate_values) * mixed.reshape(gate_values.shape)).astype(jnp.bfloat16)
    return jnp.einsum("bqc,ce->bqe", gated, out_weight, preferred_element_type=jnp.float32)


def gathered(block, axis_name):
    copies = jnp.broadcast_to(block[None], (lax.axis_size(axis_name),) + block.shape)
    return lax.all_to_all(copies, axis_name, split_axis=0, concat_axis=0, tiled=True)


def shards(
    homolog_symbol_ids,
    residue_attend_mask,
    alignment_state,
    pair,
    symbol_lookup_matrix,
    pair_bias_weight,
    row_projection_weight,
    horizontal_readout_matrix,
    column_projection_weight,
    vertical_readout_matrix,
    product_factor_matrices,
    outer_output_weight,
    triangle_input_weight,
    triangle_output_weight,
):
    residue_count = lax.axis_size("res")
    sequence_total = alignment_state.shape[0] * residue_count
    res_local = pair.shape[0]
    chain_total = pair.shape[1]
    pair_chan = pair.shape[2]
    owner_chan = pair_chan // residue_count
    outer_chan = product_factor_matrices.shape[1] // 2
    head_count = pair_bias_weight.shape[1]
    token_class_count = symbol_lookup_matrix.shape[0]
    one_hot_tokens = (
        homolog_symbol_ids[:, :, None]
        == jnp.arange(token_class_count, dtype=jnp.int32)[None, None, :]
    ).astype(jnp.bfloat16)
    alignment_initial = alignment_state.astype(jnp.float32) + jnp.einsum(
        "kly,yb->klb", one_hot_tokens, symbol_lookup_matrix, preferred_element_type=jnp.float32
    )
    pair_normed = layer_normalized(pair.astype(jnp.float32), -1).astype(jnp.bfloat16)
    bias_local = jnp.einsum(
        "ijc,ch->hij", pair_normed, pair_bias_weight, preferred_element_type=jnp.float32
    ).astype(jnp.bfloat16)
    mask_bias = (residue_attend_mask.astype(jnp.float32) - 1.0) * 10000.0
    row_input = layer_normalized(alignment_initial, -1).astype(jnp.bfloat16)
    query_tensor, key_tensor, value_tensor, gate_values = split_proj(
        row_input, row_projection_weight, head_count
    )
    bias_all = jnp.moveaxis(gathered(bias_local, "res"), 0, 1).reshape(
        head_count, chain_total, chain_total
    )
    extra_bias = bias_all.astype(jnp.float32)[None] + mask_bias[None, None, None, :]
    row_attention_update = attention_block_fn(
        query_tensor, key_tensor, value_tensor, gate_values, extra_bias, horizontal_readout_matrix
    )
    alignment_after_rows = (alignment_initial + row_attention_update).astype(jnp.bfloat16)
    alignment_columns = lax.all_to_all(
        alignment_after_rows, "res", split_axis=1, concat_axis=0, tiled=True
    )
    column_start = jnp.swapaxes(alignment_columns, 0, 1).astype(jnp.float32)
    col_in = layer_normalized(column_start, -1).astype(jnp.bfloat16)
    col_queries, col_keys, col_values, col_gating = split_proj(
        col_in, column_projection_weight, head_count
    )
    alignment_after_columns = column_start + attention_block_fn(
        col_queries, col_keys, col_values, col_gating, jnp.float32(0.0), vertical_readout_matrix
    )
    alignment_output = jnp.swapaxes(alignment_after_columns, 0, 1).astype(jnp.bfloat16)
    outer_input = layer_normalized(alignment_after_columns, -1).astype(jnp.bfloat16)
    factor_ab = jnp.einsum(
        "rsc,ce->rse", outer_input, product_factor_matrices, preferred_element_type=jnp.float32
    )
    left = factor_ab[..., :outer_chan].astype(jnp.bfloat16)
    latter_factor = (
        factor_ab[..., outer_chan:]
        .astype(jnp.bfloat16)
        .reshape(res_local, sequence_total * outer_chan)
    )
    piece = gathered(latter_factor, "res")
    count = chain_total
    right_rows = piece.reshape(count, sequence_total, outer_chan)
    cross_product_result = (
        jnp.einsum("isc,jsd->ijcd", left, right_rows, preferred_element_type=jnp.float32)
        / sequence_total
    ).astype(jnp.bfloat16)
    update = jnp.einsum(
        "ije,ez->ijz",
        cross_product_result.reshape(res_local, count, outer_chan * outer_chan),
        outer_output_weight,
        preferred_element_type=jnp.float32,
    )
    pair_one = pair.astype(jnp.float32) + update
    tri_normed = layer_normalized(pair_one, -1).astype(jnp.bfloat16)
    factors = jnp.einsum(
        "ijc,ce->eij",
        tri_normed,
        triangle_input_weight[:, : 4 * pair_chan],
        preferred_element_type=jnp.float32,
    )
    gate_out = jnp.einsum(
        "ijc,ce->ije",
        tri_normed,
        triangle_input_weight[:, 4 * pair_chan :],
        preferred_element_type=jnp.float32,
    )
    left_f = (jax.nn.sigmoid(factors[pair_chan : 2 * pair_chan]) * factors[:pair_chan]).astype(
        jnp.bfloat16
    )
    right_f = (
        jax.nn.sigmoid(factors[3 * pair_chan :]) * factors[2 * pair_chan : 3 * pair_chan]
    ).astype(jnp.bfloat16)
    left_f = left_f.reshape(residue_count, owner_chan, res_local, chain_total)
    right_f = right_f.reshape(residue_count, owner_chan, res_local, chain_total)
    both = lax.all_to_all(
        jnp.stack([left_f, right_f], 1), "res", split_axis=0, concat_axis=0, tiled=True
    )
    both = jnp.moveaxis(both, 0, 2).reshape(2, owner_chan, chain_total, chain_total)
    combined = jnp.einsum(
        "cik,cjk->cij", both[0], both[1], preferred_element_type=jnp.float32
    ).astype(jnp.bfloat16)[None]
    back_rows = lax.all_to_all(combined, "res", split_axis=2, concat_axis=0, tiled=True)
    back_rows = back_rows.reshape(pair_chan, res_local, chain_total)
    comb_normed = layer_normalized(back_rows.astype(jnp.float32), 0).astype(jnp.bfloat16)
    tri_update = jnp.einsum(
        "cij,cz->ijz", comb_normed, triangle_output_weight, preferred_element_type=jnp.float32
    )
    pair_output = (pair_one + jax.nn.sigmoid(gate_out) * tri_update).astype(jnp.bfloat16)
    return (alignment_output, pair_output)


def solution(mesh):
    placed = (
        P(("crop", "res"), None),
        P("crop"),
        P(("crop", "res"), None, None),
        P(("crop", "res"), None, None),
        P(),
        P(),
        P(),
        P(),
        P(),
        P(),
        P(),
        P(),
        P(),
        P(),
    )
    return jax.shard_map(
        shards,
        mesh=mesh,
        in_specs=placed,
        out_specs=(P("crop", "res", None), P(("crop", "res"), None, None)),
        check_vma=False,
    )
```

```python
import functools

import jax
import jax.numpy as jnp
from jax import lax
from jax.experimental import pallas as pl
from jax.experimental.pallas import tpu as pltpu
from jax.sharding import PartitionSpec as P

EPSILON = 1e-05
F32 = jnp.float32
BF16 = jnp.bfloat16
VMEM_BYTES = 48 * 1024 * 1024


def normalized(rows, axis):
    average = jnp.mean(rows, axis, keepdims=True)
    centred = rows - average
    spread = jnp.mean(centred * centred, axis, keepdims=True)
    return centred * lax.rsqrt(spread + EPSILON)


def dot(a, b):
    return jnp.dot(a, b, preferred_element_type=F32)


def dot_t(a, b):
    return lax.dot_general(a, b, (((1,), (1,)), ((), ())), preferred_element_type=F32)


def t_dot(a, b):
    return lax.dot_general(a, b, (((0,), (0,)), ((), ())), preferred_element_type=F32)


def iota(shape, axis):
    return lax.broadcasted_iota(jnp.int32, shape, axis)


def selector(size, source_of):
    shape = (size, size)
    return (iota(shape, 1) == source_of(iota(shape, 0))).astype(F32).astype(BF16)


def swapped(outer, inner):
    return lambda p: (p % outer) * inner + p // outer


def head_mask(heads, channels, lead):
    width = channels // heads
    shape = (heads, channels)
    mask = (iota(shape, 0) == iota(shape, 1) // width).astype(F32)
    return mask[None] if lead else mask


def kernel_call(body, outs, args, name, flops=0, nbytes=0):
    spec = pl.BlockSpec(memory_space=pltpu.VMEM)
    return pl.pallas_call(
        body,
        out_shape=tuple(jax.ShapeDtypeStruct(s, d) for s, d in outs),
        in_specs=[spec] * len(args),
        out_specs=(spec,) * len(outs),
        compiler_params=pltpu.CompilerParams(vmem_limit_bytes=VMEM_BYTES),
        cost_estimate=pl.CostEstimate(flops=flops, bytes_accessed=nbytes, transcendentals=0),
        name=name,
    )(*args)


def bias_kernel(pair_ref, weight_ref, out_ref):
    rows, columns, channels = pair_ref.shape
    heads = weight_ref.shape[1]
    x = pair_ref[...].reshape(rows * columns, channels).astype(F32)
    normed = normalized(x, -1).astype(BF16)
    bias = lax.dot_general(
        weight_ref[...], normed, (((0,), (1,)), ((), ())), preferred_element_type=F32
    )
    block = jnp.concatenate(
        [bias[:, i * columns : (i + 1) * columns] for i in range(rows)], 0
    ).astype(BF16)
    for d in range(out_ref.shape[0]):
        out_ref[d] = block


def row_scores_kernel(
    ids_ref, mask_ref, state_ref, table_ref, weight_ref,
    scores_ref, value_ref, gate_ref, start_ref,
    *, heads,
):
    sequences, length, channels = state_ref.shape
    tokens = table_ref.shape[0]
    starts = []
    for s in range(sequences):
        hot = (iota((tokens, length), 0) == ids_ref[s : s + 1, :]).astype(F32).astype(BF16)
        starts.append(state_ref[s].astype(F32) + t_dot(hot, table_ref[...]))
    start = jnp.concatenate(starts, 0)
    start_ref[...] = start
    projected = dot(normalized(start, -1).astype(BF16), weight_ref[...])
    query = (projected[:, :channels] * (channels // heads) ** (-0.5)).astype(BF16).astype(F32)
    key = projected[:, channels : 2 * channels].astype(BF16)
    value_ref[...] = projected[:, 2 * channels : 3 * channels].astype(BF16)
    gate_ref[...] = jax.nn.sigmoid(projected[:, 3 * channels :])
    mask = head_mask(heads, channels, True)
    extra = (mask_ref[...].astype(F32) - 1.0) * 10000.0
    for s in range(sequences):
        rows = slice(s * length, (s + 1) * length)
        spread = (query[rows][:, None, :] * mask).reshape(length * heads, channels).astype(BF16)
        scores_ref[s] = dot_t(spread, key[rows]) + extra


def softmax(scores):
    top = jnp.max(scores, -1, keepdims=True)
    e = jnp.exp(scores - top)
    return (e * (1.0 / jnp.sum(e, -1, keepdims=True))).astype(BF16)


def row_mix_kernel(
    scores_ref, bias_ref, value_ref, gate_ref, start_ref, weight_ref, out_ref, *, heads
):
    sequences, expanded, length = scores_ref.shape
    channels = value_ref.shape[1]
    devices = out_ref.shape[0]
    bias = bias_ref[...].reshape(expanded, length).astype(F32)
    mask = head_mask(heads, channels, True)
    shape = (length, expanded)
    gather = (iota(shape, 0) == iota(shape, 1) // heads).astype(F32).astype(BF16)
    mixed = []
    for s in range(sequences):
        rows = slice(s * length, (s + 1) * length)
        weights = softmax(scores_ref[s] + bias)
        whole = dot(weights, value_ref[rows])
        own = (whole.reshape(length, heads, channels) * mask).reshape(expanded, channels)
        mixed.append(dot(gather, own.astype(BF16)))
    mixed = jnp.concatenate(mixed, 0)
    gated = (gate_ref[...] * mixed).astype(BF16)
    after = (start_ref[...] + dot(gated, weight_ref[...])).astype(BF16)
    own_rows = length // devices
    size = sequences * length
    block = sequences * own_rows
    order = selector(
        size, lambda p: (p % block) // own_rows * length + p // block * own_rows + p % own_rows
    )
    out_ref[...] = dot(order, after).astype(BF16).reshape(out_ref.shape)


def column_kernel(
    state_ref, weight_ref, readout_ref, factor_ref, out_ref, left_ref, right_ref, *, heads, own_rows
):
    devices, block, channels = state_ref.shape
    size = devices * block
    sequences = size // own_rows
    to_rows = selector(size, swapped(sequences, own_rows))
    to_sequences = selector(size, swapped(own_rows, sequences))
    start = state_ref[...].reshape(size, channels).astype(F32)
    normed = dot(to_rows, normalized(start, -1).astype(BF16)).astype(BF16)
    projected = dot(normed, weight_ref[...])
    query = (projected[:, :channels] * (channels // heads) ** (-0.5)).astype(BF16).astype(F32)
    key = projected[:, channels : 2 * channels].astype(BF16)
    value = projected[:, 2 * channels : 3 * channels].astype(BF16)
    gate = jax.nn.sigmoid(projected[:, 3 * channels :])
    mask = head_mask(heads, channels, False)
    gated = []
    for r in range(own_rows):
        rows = slice(r * sequences, (r + 1) * sequences)
        spread = jnp.concatenate(
            [(query[rows] * mask[h : h + 1]).astype(BF16) for h in range(heads)], 0
        )
        whole = dot(softmax(dot_t(spread, key[rows])), value[rows])
        mixed = whole[:sequences] * mask[:1]
        for h in range(1, heads):
            mixed += whole[h * sequences : (h + 1) * sequences] * mask[h : h + 1]
        gated.append((gate[rows] * mixed).astype(BF16))
    gated = dot(to_sequences, jnp.concatenate(gated, 0)).astype(BF16)
    after = start + dot(gated, readout_ref[...])
    out_ref[...] = after.astype(BF16).reshape(out_ref.shape)
    normed = dot(to_rows, normalized(after, -1).astype(BF16)).astype(BF16)
    width = factor_ref.shape[1] // 2
    left_ref[...] = dot(normed, factor_ref[:, :width]).astype(BF16)
    fold = max(1, 128 // sequences)
    part = width // fold
    pieces = []
    for r in range(own_rows):
        right = lax.dot_general(
            factor_ref[:, width:],
            normed[r * sequences : (r + 1) * sequences],
            (((0,), (1,)), ((), ())),
            preferred_element_type=F32,
        )
        pieces.append(
            jnp.concatenate([right[f * part : (f + 1) * part] for f in range(fold)], 1)
        )
    pieces = jnp.concatenate(pieces, 0).astype(BF16)
    pieces = dot(selector(own_rows * part, swapped(own_rows, part)), pieces)
    lanes = fold * sequences
    packed = jnp.concatenate(
        [pieces[q * own_rows : (q + 1) * own_rows] for q in range(part)], 1
    ).astype(BF16)
    for d in range(right_ref.shape[0]):
        right_ref[d] = packed


def spread_kernel(left_ref, weight_ref, out_ref, *, own_rows):
    size, width = left_ref.shape
    sequences = size // own_rows
    channels = weight_ref.shape[1] // width
    fold = max(1, 128 // sequences)
    part = width // fold
    product = dot(left_ref[...], weight_ref[...])
    for d in range(width):
        at = (d % part * fold + d // part) * sequences
        for r in range(own_rows):
            out_ref[at : at + sequences, r * channels : (r + 1) * channels] = product[
                r * sequences : (r + 1) * sequences, d * channels : (d + 1) * channels
            ].astype(BF16)


def pair_kernel(
    right_ref, spread_ref, pair_ref, weight_ref, one_ref, normed_ref, out_ref, *, sequences
):
    own_rows, columns, channels = pair_ref.shape
    right = right_ref[...].reshape(columns, right_ref.shape[-1])
    update = dot(right, spread_ref[...]) * (1.0 / sequences)
    ones = [
        pair_ref[i].astype(F32) + update[:, i * channels : (i + 1) * channels]
        for i in range(own_rows)
    ]
    one = jnp.concatenate(ones, 0)
    one_ref[...] = one
    normed = normalized(one, -1).astype(BF16)
    normed_ref[...] = normed
    factors = dot_t(weight_ref[...], normed)
    left = jax.nn.sigmoid(factors[channels : 2 * channels]) * factors[:channels]
    right = jax.nn.sigmoid(factors[3 * channels :]) * factors[2 * channels : 3 * channels]
    both = jnp.concatenate([left.astype(BF16), right.astype(BF16)], 1)
    out_ref[...] = both.reshape(out_ref.shape)


def gate_kernel(normed_ref, weight_ref, out_ref):
    out_ref[...] = jax.nn.sigmoid(dot(normed_ref[...], weight_ref[...]))


def triangle_kernel(both_ref, out_ref, *, own_rows):
    devices, own_channels, lanes = both_ref.shape
    columns = lanes // 2 // own_rows
    size = devices * own_channels
    both = both_ref[...].reshape(size, lanes)
    left = jnp.concatenate([both[:, i * columns : (i + 1) * columns] for i in range(own_rows)], 0)
    right = jnp.concatenate(
        [both[:, (own_rows + i) * columns : (own_rows + i + 1) * columns] for i in range(own_rows)],
        0,
    )
    total = size * own_rows
    order = selector(
        total,
        lambda p: p % own_rows * size + p % columns // own_rows * own_channels + p // columns,
    )
    right = dot(order, right).astype(BF16)
    channel = iota((total, 1), 0) % own_channels
    combined = jnp.zeros((total, columns), F32)
    for c in range(own_channels):
        part = dot_t(left, right[c * columns : (c + 1) * columns])
        combined = jnp.where(channel == c, part, combined)
    combined = combined.astype(BF16)
    out_ref[...] = jnp.concatenate(
        [combined[i * size : (i + 1) * size] for i in range(own_rows)], 1
    ).reshape(out_ref.shape)


def final_kernel(back_ref, one_ref, gate_ref, weight_ref, out_ref):
    channels = weight_ref.shape[0]
    combined = back_ref[...].reshape(channels, back_ref.shape[-1]).astype(F32)
    normed = normalized(combined, 0).astype(BF16)
    update = t_dot(normed, weight_ref[...])
    out_ref[...] = (one_ref[...] + gate_ref[...] * update).astype(BF16).reshape(out_ref.shape)


def exchanged(x):
    return lax.all_to_all(x, "res", split_axis=0, concat_axis=0, tiled=True)


def shards(
    homolog_symbol_ids,
    residue_attend_mask,
    alignment_state,
    pair,
    symbol_lookup_matrix,
    pair_bias_weight,
    row_projection_weight,
    horizontal_readout_matrix,
    column_projection_weight,
    vertical_readout_matrix,
    product_factor_matrices,
    outer_output_weight,
    triangle_input_weight,
    triangle_output_weight,
):
    devices = lax.axis_size("res")
    own_sequences, length, channels = alignment_state.shape
    sequences = own_sequences * devices
    own_rows, columns, pair_channels = pair.shape
    heads = pair_bias_weight.shape[1]
    width = product_factor_matrices.shape[1] // 2
    own_channels = pair_channels // devices
    rows = own_sequences * length

    (bias,) = kernel_call(
        bias_kernel,
        [((devices, own_rows * heads, columns), BF16)],
        (pair, pair_bias_weight),
        "bias",
    )
    bias = exchanged(bias)
    scores, value, gate, start = kernel_call(
        functools.partial(row_scores_kernel, heads=heads),
        [
            ((own_sequences, length * heads, length), F32),
            ((rows, channels), BF16),
            ((rows, channels), F32),
            ((rows, channels), F32),
        ],
        (
            homolog_symbol_ids,
            residue_attend_mask.reshape(1, length),
            alignment_state,
            symbol_lookup_matrix,
            row_projection_weight,
        ),
        "row_scores",
        flops=2 * rows * channels * 4 * channels,
        nbytes=1 << 21,
    )
    (after_rows,) = kernel_call(
        functools.partial(row_mix_kernel, heads=heads),
        [((devices, own_sequences * own_rows, channels), BF16)],
        (scores, bias, value, gate, start, horizontal_readout_matrix),
        "row_mix",
    )
    by_residue = exchanged(after_rows)
    alignment_output, left, right = kernel_call(
        functools.partial(column_kernel, heads=heads, own_rows=own_rows),
        [
            ((sequences, own_rows, channels), BF16),
            ((sequences * own_rows, width), BF16),
            ((devices, own_rows, width * sequences), BF16),
        ],
        (
            by_residue,
            column_projection_weight,
            vertical_readout_matrix,
            product_factor_matrices,
        ),
        "column",
    )
    right = exchanged(right)
    (spread,) = kernel_call(
        functools.partial(spread_kernel, own_rows=own_rows),
        [((width * sequences, own_rows * pair_channels), BF16)],
        (left, outer_output_weight.reshape(width, width * pair_channels)),
        "spread",
        flops=2 * own_rows * sequences * width * width * pair_channels,
        nbytes=1 << 21,
    )
    pair_one, normed, both = kernel_call(
        functools.partial(pair_kernel, sequences=sequences),
        [
            ((own_rows * columns, pair_channels), F32),
            ((own_rows * columns, pair_channels), BF16),
            ((devices, own_channels, 2 * own_rows * columns), BF16),
        ],
        (right, spread, pair, triangle_input_weight[:, : 4 * pair_channels].T),
        "pair",
    )
    both = exchanged(both)
    (gate_out,) = kernel_call(
        gate_kernel,
        [((own_rows * columns, pair_channels), F32)],
        (normed, triangle_input_weight[:, 4 * pair_channels :]),
        "gate",
        flops=2 * own_rows * columns * pair_channels * pair_channels,
        nbytes=1 << 19,
    )
    (combined,) = kernel_call(
        functools.partial(triangle_kernel, own_rows=own_rows),
        [((devices, own_channels, own_rows * columns), BF16)],
        (both,),
        "triangle",
    )
    back = exchanged(combined)
    (pair_output,) = kernel_call(
        final_kernel,
        [((own_rows, columns, pair_channels), BF16)],
        (back, pair_one, gate_out, triangle_output_weight),
        "final",
    )
    return (alignment_output, pair_output)


def solution(mesh):
    placed = (
        P(("crop", "res"), None),
        P("crop"),
        P(("crop", "res"), None, None),
        P(("crop", "res"), None, None),
    ) + (P(),) * 10
    return jax.shard_map(
        shards,
        mesh=mesh,
        in_specs=placed,
        out_specs=(P("crop", "res", None), P(("crop", "res"), None, None)),
        check_vma=False,
    )
```

```python
import functools

import jax
import jax.numpy as jnp
from jax import lax
from jax.experimental import pallas as pl
from jax.experimental.pallas import tpu as pltpu
from jax.sharding import PartitionSpec as P

EPSILON = 1e-05
F32 = jnp.float32
BF16 = jnp.bfloat16
VMEM_BYTES = 48 * 1024 * 1024


def normalized(rows, axis):
    average = jnp.mean(rows, axis, keepdims=True)
    centred = rows - average
    spread = jnp.mean(centred * centred, axis, keepdims=True)
    return centred * lax.rsqrt(spread + EPSILON)


def dot(a, b):
    return jnp.dot(a, b, preferred_element_type=F32)


def dot_t(a, b):
    return lax.dot_general(a, b, (((1,), (1,)), ((), ())), preferred_element_type=F32)


def t_dot(a, b):
    return lax.dot_general(a, b, (((0,), (0,)), ((), ())), preferred_element_type=F32)


def iota(shape, axis):
    return lax.broadcasted_iota(jnp.int32, shape, axis)


def selector(size, source_of):
    shape = (size, size)
    return (iota(shape, 1) == source_of(iota(shape, 0))).astype(F32).astype(BF16)


def swapped(outer, inner):
    return lambda p: (p % outer) * inner + p // outer


def head_mask(heads, channels, lead):
    width = channels // heads
    shape = (heads, channels)
    mask = (iota(shape, 0) == iota(shape, 1) // width).astype(F32)
    return mask[None] if lead else mask


def kernel_call(body, outs, args, name, flops=0, nbytes=0, scalars=0):
    spec = pl.BlockSpec(memory_space=pltpu.VMEM)
    scalar = pl.BlockSpec(memory_space=pltpu.SMEM)
    return pl.pallas_call(
        body,
        out_shape=tuple(jax.ShapeDtypeStruct(s, d) for s, d in outs),
        in_specs=[scalar] * scalars + [spec] * (len(args) - scalars),
        out_specs=(spec,) * len(outs),
        compiler_params=pltpu.CompilerParams(vmem_limit_bytes=VMEM_BYTES),
        cost_estimate=pl.CostEstimate(flops=flops, bytes_accessed=nbytes, transcendentals=0),
        name=name,
    )(*args)


def bias_kernel(pair_hbm, weight_hbm, out_ref, pair_ref, weight_ref, sems):
    rows = pair_ref.shape[0]
    copies = [pltpu.make_async_copy(weight_hbm, weight_ref, sems.at[rows])] + [
        pltpu.make_async_copy(pair_hbm.at[i], pair_ref.at[i], sems.at[i]) for i in range(rows)
    ]
    for copy in copies:
        copy.start()
    for copy in copies:
        copy.wait()
    _, columns, channels = pair_ref.shape
    x = pair_ref[...].reshape(rows * columns, channels).astype(F32)
    bias = dot_t(weight_ref[...], normalized(x, -1).astype(BF16))
    block = jnp.concatenate(
        [bias[:, i * columns : (i + 1) * columns] for i in range(rows)], 0
    ).astype(BF16)
    for d in range(out_ref.shape[0]):
        out_ref[d] = block


def row_scores_kernel(
    ids_ref, mask_ref, state_ref, table_ref, weight_ref, readout_ref,
    scores_ref, value_ref, gate_ref, start_ref, held_ref,
    *, heads,
):
    sequences, length, channels = state_ref.shape
    tokens = table_ref.shape[0]
    held_ref[...] = readout_ref[...]
    starts = []
    for s in range(sequences):
        hot = (iota((tokens, length), 0) == ids_ref[s : s + 1, :]).astype(F32).astype(BF16)
        starts.append(state_ref[s].astype(F32) + t_dot(hot, table_ref[...]))
    start = jnp.concatenate(starts, 0)
    start_ref[...] = start
    projected = dot(normalized(start, -1).astype(BF16), weight_ref[...])
    query = (projected[:, :channels] * (channels // heads) ** (-0.5)).astype(BF16).astype(F32)
    key = projected[:, channels : 2 * channels].astype(BF16)
    value_ref[...] = projected[:, 2 * channels : 3 * channels].astype(BF16)
    gate_ref[...] = jax.nn.sigmoid(projected[:, 3 * channels :])
    mask = head_mask(heads, channels, True)
    extra = (mask_ref[...].astype(F32) - 1.0) * 10000.0
    for s in range(sequences):
        rows = slice(s * length, (s + 1) * length)
        spread = (query[rows][:, None, :] * mask).reshape(length * heads, channels).astype(BF16)
        scores_ref[s] = dot_t(spread, key[rows]) + extra


def softmax(scores):
    top = jnp.max(scores, -1, keepdims=True)
    e = jnp.exp(scores - top)
    return (e * (1.0 / jnp.sum(e, -1, keepdims=True))).astype(BF16)


def row_mix_kernel(
    scores_ref, bias_ref, value_ref, gate_ref, start_ref, weight_ref, out_ref, *, heads
):
    sequences, expanded, length = scores_ref.shape
    channels = value_ref.shape[1]
    devices = out_ref.shape[0]
    bias = bias_ref[...].reshape(expanded, length).astype(F32)
    mask = head_mask(heads, channels, True)
    shape = (length, expanded)
    gather = (iota(shape, 0) == iota(shape, 1) // heads).astype(F32).astype(BF16)
    mixed = []
    for s in range(sequences):
        rows = slice(s * length, (s + 1) * length)
        weights = softmax(scores_ref[s] + bias)
        whole = dot(weights, value_ref[rows])
        own = (whole.reshape(length, heads, channels) * mask).reshape(expanded, channels)
        mixed.append(dot(gather, own.astype(BF16)))
    mixed = jnp.concatenate(mixed, 0)
    gated = (gate_ref[...] * mixed).astype(BF16)
    after = (start_ref[...] + dot(gated, weight_ref[...])).astype(BF16)
    own_rows = length // devices
    size = sequences * length
    block = sequences * own_rows
    order = selector(
        size, lambda p: (p % block) // own_rows * length + p // block * own_rows + p % own_rows
    )
    out_ref[...] = dot(order, after).astype(BF16).reshape(out_ref.shape)


def column_kernel(
    state_ref, weight_ref, readout_ref, factor_ref, out_ref, left_ref, right_ref, *, heads, own_rows
):
    devices, block, channels = state_ref.shape
    size = devices * block
    sequences = size // own_rows
    to_rows = selector(size, swapped(sequences, own_rows))
    to_sequences = selector(size, swapped(own_rows, sequences))
    start = state_ref[...].reshape(size, channels).astype(F32)
    normed = dot(to_rows, normalized(start, -1).astype(BF16)).astype(BF16)
    projected = dot(normed, weight_ref[...])
    query = (projected[:, :channels] * (channels // heads) ** (-0.5)).astype(BF16).astype(F32)
    key = projected[:, channels : 2 * channels].astype(BF16)
    value = projected[:, 2 * channels : 3 * channels].astype(BF16)
    gate = jax.nn.sigmoid(projected[:, 3 * channels :])
    mask = head_mask(heads, channels, False)
    gated = []
    for r in range(own_rows):
        rows = slice(r * sequences, (r + 1) * sequences)
        spread = jnp.concatenate(
            [(query[rows] * mask[h : h + 1]).astype(BF16) for h in range(heads)], 0
        )
        whole = dot(softmax(dot_t(spread, key[rows])), value[rows])
        mixed = whole[:sequences] * mask[:1]
        for h in range(1, heads):
            mixed += whole[h * sequences : (h + 1) * sequences] * mask[h : h + 1]
        gated.append((gate[rows] * mixed).astype(BF16))
    gated = dot(to_sequences, jnp.concatenate(gated, 0)).astype(BF16)
    after = start + dot(gated, readout_ref[...])
    out_ref[...] = after.astype(BF16).reshape(out_ref.shape)
    normed = dot(to_rows, normalized(after, -1).astype(BF16)).astype(BF16)
    width = factor_ref.shape[0] // 2
    left_ref[...] = dot_t(normed, factor_ref[:width]).astype(BF16)
    fold = max(1, 128 // sequences)
    part = width // fold
    pieces = []
    for r in range(own_rows):
        right = dot_t(factor_ref[width:], normed[r * sequences : (r + 1) * sequences])
        pieces.append(
            jnp.concatenate([right[f * part : (f + 1) * part] for f in range(fold)], 1)
        )
    pieces = jnp.concatenate(pieces, 0).astype(BF16)
    pieces = dot(selector(own_rows * part, swapped(own_rows, part)), pieces)
    packed = jnp.concatenate(
        [pieces[q * own_rows : (q + 1) * own_rows] for q in range(part)], 1
    ).astype(BF16)
    for d in range(right_ref.shape[0]):
        right_ref[d] = packed


def spread_kernel(left_ref, weight_ref, out_ref, *, own_rows):
    size, width = left_ref.shape
    sequences = size // own_rows
    channels = weight_ref.shape[1] // width
    fold = max(1, 128 // sequences)
    part = width // fold
    product = dot(left_ref[...], weight_ref[...])
    for d in range(width):
        at = (d % part * fold + d // part) * sequences
        for r in range(own_rows):
            out_ref[at : at + sequences, r * channels : (r + 1) * channels] = product[
                r * sequences : (r + 1) * sequences, d * channels : (d + 1) * channels
            ].astype(BF16)


def pair_kernel(
    second_ref, right_ref, other_ref, spread_ref, pair_ref, weight_ref, gate_weight_ref,
    one_ref, gate_ref, out_ref,
    *, sequences,
):
    own_rows, columns, channels = pair_ref.shape
    flip = jnp.full(right_ref.shape, second_ref[0], jnp.int32) == 1
    mine, other = right_ref[...].astype(F32), other_ref[...].astype(F32)
    right = jnp.concatenate([jnp.where(flip, other, mine), jnp.where(flip, mine, other)], 1)
    right = right.reshape(columns, right_ref.shape[-1]).astype(BF16)
    update = dot(right, spread_ref[...]) * (1.0 / sequences)
    ones = [
        pair_ref[i].astype(F32) + update[:, i * channels : (i + 1) * channels]
        for i in range(own_rows)
    ]
    one = jnp.concatenate(ones, 0)
    one_ref[...] = one
    normed = normalized(one, -1).astype(BF16)
    gate_ref[...] = jax.nn.sigmoid(dot(normed, gate_weight_ref[...]))
    factors = dot_t(weight_ref[...], normed)
    left = jax.nn.sigmoid(factors[channels : 2 * channels]) * factors[:channels]
    right = jax.nn.sigmoid(factors[3 * channels :]) * factors[2 * channels : 3 * channels]
    both = jnp.concatenate([left.astype(BF16), right.astype(BF16)], 1)
    out_ref[...] = both.reshape(out_ref.shape)


def triangle_kernel(both_ref, out_ref, *, own_rows):
    devices, own_channels, lanes = both_ref.shape
    columns = lanes // 2 // own_rows
    size = devices * own_channels
    both = both_ref[...].reshape(size, lanes)
    left = jnp.concatenate([both[:, i * columns : (i + 1) * columns] for i in range(own_rows)], 0)
    right = jnp.concatenate(
        [both[:, (own_rows + i) * columns : (own_rows + i + 1) * columns] for i in range(own_rows)],
        0,
    )
    total = size * own_rows
    order = selector(
        total,
        lambda p: p % own_rows * size + p % columns // own_rows * own_channels + p // columns,
    )
    right = dot(order, right).astype(BF16)
    channel = iota((total, 1), 0) % own_channels
    combined = jnp.zeros((total, columns), F32)
    for c in range(own_channels):
        part = dot_t(left, right[c * columns : (c + 1) * columns])
        combined = jnp.where(channel == c, part, combined)
    combined = combined.astype(BF16)
    out_ref[...] = jnp.concatenate(
        [combined[i * size : (i + 1) * size] for i in range(own_rows)], 1
    ).reshape(out_ref.shape)


def final_kernel(back_ref, one_ref, gate_ref, weight_ref, out_ref):
    channels = weight_ref.shape[0]
    combined = back_ref[...].reshape(channels, back_ref.shape[-1]).astype(F32)
    normed = normalized(combined, 0).astype(BF16)
    update = t_dot(normed, weight_ref[...])
    out_ref[...] = (one_ref[...] + gate_ref[...] * update).astype(BF16).reshape(out_ref.shape)


def exchanged(x):
    return lax.all_to_all(x, "res", split_axis=0, concat_axis=0, tiled=True)


def shards(
    homolog_symbol_ids,
    residue_attend_mask,
    alignment_state,
    pair,
    symbol_lookup_matrix,
    pair_bias_weight,
    row_projection_weight,
    horizontal_readout_matrix,
    column_projection_weight,
    vertical_readout_matrix,
    product_factor_matrices,
    outer_output_weight,
    triangle_input_weight,
    triangle_output_weight,
):
    devices = lax.axis_size("res")
    own_sequences, length, channels = alignment_state.shape
    sequences = own_sequences * devices
    own_rows, columns, pair_channels = pair.shape
    heads = pair_bias_weight.shape[1]
    width = product_factor_matrices.shape[1] // 2
    own_channels = pair_channels // devices
    rows = own_sequences * length

    outside = pl.BlockSpec(memory_space=pl.ANY)
    bias = pl.pallas_call(
        bias_kernel,
        out_shape=jax.ShapeDtypeStruct((devices, own_rows * heads, columns), BF16),
        in_specs=[outside, outside],
        out_specs=pl.BlockSpec(memory_space=pltpu.VMEM),
        scratch_shapes=[
            pltpu.VMEM(pair.shape, BF16),
            pltpu.VMEM(pair_bias_weight.shape[::-1], BF16),
            pltpu.SemaphoreType.DMA((own_rows + 1,)),
        ],
        name="bias",
    )(pair, pair_bias_weight.T)
    bias = exchanged(bias)
    scores, value, gate, start, readout = kernel_call(
        functools.partial(row_scores_kernel, heads=heads),
        [
            ((own_sequences, length * heads, length), F32),
            ((rows, channels), BF16),
            ((rows, channels), F32),
            ((rows, channels), F32),
            ((channels, channels), BF16),
        ],
        (
            homolog_symbol_ids,
            residue_attend_mask.reshape(1, length),
            alignment_state,
            symbol_lookup_matrix,
            row_projection_weight,
            horizontal_readout_matrix,
        ),
        "row_scores",
        flops=2 * rows * channels * 4 * channels,
        nbytes=1 << 21,
    )
    (after_rows,) = kernel_call(
        functools.partial(row_mix_kernel, heads=heads),
        [((devices, own_sequences * own_rows, channels), BF16)],
        (scores, bias, value, gate, start, readout),
        "row_mix",
    )
    by_residue = exchanged(after_rows)
    alignment_output, left, right = kernel_call(
        functools.partial(column_kernel, heads=heads, own_rows=own_rows),
        [
            ((sequences, own_rows, channels), BF16),
            ((sequences * own_rows, width), BF16),
            ((devices // 2, own_rows, width * sequences), BF16),
        ],
        (
            by_residue,
            column_projection_weight,
            vertical_readout_matrix,
            product_factor_matrices.T,
        ),
        "column",
    )
    groups = [list(range(first, devices, 2)) for first in range(2)]
    right = lax.all_to_all(right, "res", 0, 0, axis_index_groups=groups, tiled=True)
    other = lax.ppermute(right, "res", [(i, i ^ 1) for i in range(devices)])
    second = (lax.axis_index("res") % 2).reshape(1)
    (spread,) = kernel_call(
        functools.partial(spread_kernel, own_rows=own_rows),
        [((width * sequences, own_rows * pair_channels), BF16)],
        (left, outer_output_weight.reshape(width, width * pair_channels)),
        "spread",
        flops=2 * own_rows * sequences * width * width * pair_channels,
        nbytes=1 << 21,
    )
    pair_one, gate_out, both = kernel_call(
        functools.partial(pair_kernel, sequences=sequences),
        [
            ((own_rows * columns, pair_channels), F32),
            ((own_rows * columns, pair_channels), F32),
            ((devices, own_channels, 2 * own_rows * columns), BF16),
        ],
        (
            second,
            right,
            other,
            spread,
            pair,
            triangle_input_weight[:, : 4 * pair_channels].T,
            triangle_input_weight[:, 4 * pair_channels :],
        ),
        "pair",
        scalars=1,
    )
    both = exchanged(both)
    (combined,) = kernel_call(
        functools.partial(triangle_kernel, own_rows=own_rows),
        [((devices, own_channels, own_rows * columns), BF16)],
        (both,),
        "triangle",
    )
    back = exchanged(combined)
    (pair_output,) = kernel_call(
        final_kernel,
        [((own_rows, columns, pair_channels), BF16)],
        (back, pair_one, gate_out, triangle_output_weight),
        "final",
    )
    return (alignment_output, pair_output)


def solution(mesh):
    placed = (
        P(("crop", "res"), None),
        P("crop"),
        P(("crop", "res"), None, None),
        P(("crop", "res"), None, None),
    ) + (P(),) * 10
    return jax.shard_map(
        shards,
        mesh=mesh,
        in_specs=placed,
        out_specs=(P("crop", "res", None), P(("crop", "res"), None, None)),
        check_vma=False,
    )
```

```python
import functools

import jax
import jax.numpy as jnp
from jax import lax
from jax.experimental import pallas as pl
from jax.experimental.pallas import tpu as pltpu
from jax.sharding import PartitionSpec as P

EPSILON = 1e-05
F32 = jnp.float32
BF16 = jnp.bfloat16
VMEM_BYTES = 48 * 1024 * 1024


def normalized(rows, axis):
    average = jnp.mean(rows, axis, keepdims=True)
    centred = rows - average
    spread = jnp.mean(centred * centred, axis, keepdims=True)
    return centred * lax.rsqrt(spread + EPSILON)


def dot(a, b):
    return jnp.dot(a, b, preferred_element_type=F32)


def dot_t(a, b):
    return lax.dot_general(a, b, (((1,), (1,)), ((), ())), preferred_element_type=F32)


def t_dot(a, b):
    return lax.dot_general(a, b, (((0,), (0,)), ((), ())), preferred_element_type=F32)


def iota(shape, axis):
    return lax.broadcasted_iota(jnp.int32, shape, axis)


def selector(size, source_of):
    shape = (size, size)
    return (iota(shape, 1) == source_of(iota(shape, 0))).astype(F32).astype(BF16)


def swapped(outer, inner):
    return lambda p: (p % outer) * inner + p // outer


def head_mask(heads, channels, lead):
    width = channels // heads
    shape = (heads, channels)
    mask = (iota(shape, 0) == iota(shape, 1) // width).astype(F32)
    return mask[None] if lead else mask


def kernel_call(body, outs, args, name, flops=0, nbytes=0, scalars=0, fetched=()):
    inside = pl.BlockSpec(memory_space=pltpu.VMEM)
    outside = pl.BlockSpec(memory_space=pl.ANY)
    scalar = pl.BlockSpec(memory_space=pltpu.SMEM)
    args = [
        pltpu.with_memory_space_constraint(a, pltpu.HBM) if i in fetched else a
        for i, a in enumerate(args)
    ]

    def fetching(*refs):
        refs, held, sems = list(refs[: len(args) + len(outs)]), refs[len(args) + len(outs) : -1], refs[-1]
        copies = []
        for k, i in enumerate(fetched):
            copies.append(pltpu.make_async_copy(refs[i], held[k], sems.at[k]))
            copies[-1].start()
            refs[i] = held[k]
        for copy in copies:
            copy.wait()
        body(*refs)

    scratch = [pltpu.VMEM(args[i].shape, args[i].dtype) for i in fetched]
    return pl.pallas_call(
        fetching if fetched else body,
        out_shape=tuple(jax.ShapeDtypeStruct(s, d) for s, d in outs),
        in_specs=[
            scalar if i < scalars else outside if i in fetched else inside
            for i in range(len(args))
        ],
        out_specs=(inside,) * len(outs),
        scratch_shapes=scratch + [pltpu.SemaphoreType.DMA((len(fetched),))] if fetched else [],
        compiler_params=pltpu.CompilerParams(vmem_limit_bytes=VMEM_BYTES),
        cost_estimate=pl.CostEstimate(flops=flops, bytes_accessed=nbytes, transcendentals=0),
        name=name,
    )(*args)


def bias_kernel(pair_ref, weight_ref, out_ref):
    rows, columns, channels = pair_ref.shape
    x = pair_ref[...].reshape(rows * columns, channels).astype(F32)
    bias = dot_t(weight_ref[...], normalized(x, -1).astype(BF16))
    block = jnp.concatenate(
        [bias[:, i * columns : (i + 1) * columns] for i in range(rows)], 0
    ).astype(BF16)
    for d in range(out_ref.shape[0]):
        out_ref[d] = block


def ordered(second, mine, other):
    flip = jnp.full(mine.shape, second, jnp.int32) == 1
    return jnp.where(flip, other, mine), jnp.where(flip, mine, other)


def row_scores_kernel(
    second_ref, ids_ref, other_ids_ref, mask_ref, state_ref, other_ref, table_ref, weight_ref,
    readout_ref, factor_ref,
    scores_ref, value_ref, gate_ref, start_ref, held_ref, wide_ref,
    *, heads, own_rows,
):
    own_sequences, length, channels = state_ref.shape
    tokens = table_ref.shape[0]
    second = second_ref[0]
    held_ref[...] = readout_ref[...]
    ids = jnp.concatenate(ordered(second, ids_ref[...], other_ids_ref[...]), 0)
    states = jnp.concatenate(
        ordered(second, state_ref[...].astype(F32), other_ref[...].astype(F32)), 0
    )
    sequences = 2 * own_sequences
    starts = []
    for s in range(sequences):
        hot = (iota((tokens, length), 0) == ids[s : s + 1, :]).astype(F32).astype(BF16)
        starts.append(states[s] + t_dot(hot, table_ref[...]))
    start = jnp.concatenate(starts, 0)
    normed = normalized(start, -1)
    projected = dot(normed.astype(BF16), weight_ref[:, channels : 3 * channels])
    key = projected[:, :channels].astype(BF16)
    value_ref[...] = projected[:, channels:].astype(BF16)

    def mine(x):
        pairs = x.reshape(sequences * length // (2 * own_rows), 2 * own_rows, channels)
        low, high = pairs[:, :own_rows], pairs[:, own_rows:]
        return ordered(second, low, high)[0].reshape(sequences * length // 2, channels)

    start_ref[...] = mine(start)
    own = mine(normed).astype(BF16)
    query = dot(own, weight_ref[:, :channels]) * (channels // heads) ** (-0.5)
    query = query.astype(BF16).astype(F32)
    gate_ref[...] = jax.nn.sigmoid(dot(own, weight_ref[:, 3 * channels :]))
    mask = head_mask(heads, channels, True)
    extra = (mask_ref[...].astype(F32) - 1.0) * 10000.0
    half = length // 2
    for s in range(sequences):
        rows = query[s * half : (s + 1) * half]
        spread = (rows[:, None, :] * mask).reshape(half * heads, channels).astype(BF16)
        scores_ref[s] = dot_t(spread, key[s * length : (s + 1) * length]) + extra
    width = factor_ref.shape[0] // 2
    right = factor_ref[width:].astype(F32)
    repeated = jnp.broadcast_to(right[:, None, :], (width, own_rows, channels)).reshape(
        width * own_rows, channels
    )
    row = iota(repeated.shape, 0) % own_rows
    for r in range(own_rows):
        wide_ref[:, r * channels : (r + 1) * channels] = jnp.where(row == r, repeated, 0.0).astype(
            BF16
        )


def softmax_parts(scores):
    e = jnp.exp(scores - jnp.max(scores, -1, keepdims=True))
    return e.astype(BF16), 1.0 / jnp.sum(e, -1, keepdims=True)


def row_mix_kernel(
    scores_ref, bias_ref, value_ref, gate_ref, start_ref, weight_ref, out_ref, *, heads
):
    sequences, expanded, length = scores_ref.shape
    channels = value_ref.shape[1]
    devices = out_ref.shape[0]
    rows = expanded // heads
    bias = bias_ref[...].reshape(expanded, length).astype(F32)
    mask = head_mask(heads, channels, True)
    shape = (rows, expanded)
    gather = (iota(shape, 0) == iota(shape, 1) // heads).astype(F32).astype(BF16)
    mixed = []
    for s in range(sequences):
        weights, scale = softmax_parts(scores_ref[s] + bias)
        whole = dot(weights, value_ref[s * length : (s + 1) * length]) * scale
        own = (whole.reshape(rows, heads, channels) * mask).reshape(expanded, channels)
        mixed.append(dot(gather, own.astype(BF16)))
    mixed = jnp.concatenate(mixed, 0)
    gated = (gate_ref[...] * mixed).astype(BF16)
    after = start_ref[...] + dot(gated, weight_ref[...])
    blocks = [
        after[s * rows : (s + 1) * rows].reshape(devices, rows // devices, channels)
        for s in range(sequences)
    ]
    out_ref[...] = jnp.concatenate(blocks, 1).astype(BF16)


def column_kernel(
    state_ref, weight_ref, readout_ref, factor_ref, wide_ref, out_ref, left_ref, right_ref,
    *, heads, own_rows,
):
    devices, block, channels = state_ref.shape
    size = devices * block
    sequences = size // own_rows
    to_rows = selector(size, swapped(sequences, own_rows))
    to_sequences = selector(size, swapped(own_rows, sequences))
    start = dot(to_rows, state_ref[...].reshape(size, channels))
    projected = dot(normalized(start, -1).astype(BF16), weight_ref[...])
    query = (projected[:, :channels] * (channels // heads) ** (-0.5)).astype(BF16).astype(F32)
    key = projected[:, channels : 2 * channels].astype(BF16)
    value = projected[:, 2 * channels : 3 * channels].astype(BF16)
    gate = jax.nn.sigmoid(projected[:, 3 * channels :])
    mask = head_mask(heads, channels, False)
    gated = []
    for r in range(own_rows):
        rows = slice(r * sequences, (r + 1) * sequences)
        spread = jnp.concatenate(
            [(query[rows] * mask[h : h + 1]).astype(BF16) for h in range(heads)], 0
        )
        weights, scale = softmax_parts(dot_t(spread, key[rows]))
        whole = dot(weights, value[rows]) * scale
        mixed = whole[:sequences] * mask[:1]
        for h in range(1, heads):
            mixed += whole[h * sequences : (h + 1) * sequences] * mask[h : h + 1]
        gated.append((gate[rows] * mixed).astype(BF16))
    after = start + dot(jnp.concatenate(gated, 0), readout_ref[...])
    normed = normalized(after, -1).astype(BF16)
    width = factor_ref.shape[0] // 2
    fold = max(1, 128 // sequences)
    part = width // fold
    side = jnp.concatenate(
        [normed[r * sequences : (r + 1) * sequences] for r in range(own_rows)], 1
    )
    right = dot_t(wide_ref[...], side)
    cut = part * own_rows
    right = jnp.concatenate([right[f * cut : (f + 1) * cut] for f in range(fold)], 1)
    tall = right_ref.shape[1]
    packed = jnp.concatenate(
        [right[t * tall : (t + 1) * tall] for t in range(cut // tall)], 1
    ).astype(BF16)
    for d in range(right_ref.shape[0]):
        right_ref[d] = packed
    left_ref[...] = dot_t(normed, factor_ref[:width]).astype(BF16)
    out_ref[...] = dot(to_sequences, after.astype(BF16)).astype(BF16).reshape(out_ref.shape)


def spread_kernel(aligned_ref, left_ref, weight_ref, out_ref, final_ref, sem, *, own_rows, per):
    store = pltpu.make_async_copy(aligned_ref, final_ref, sem)
    store.start()
    size, width = left_ref.shape
    sequences = size // own_rows
    channels = weight_ref.shape[1] // width
    fold = max(1, 128 // sequences)
    part = width // fold
    product = dot(left_ref[...], weight_ref[...])
    for d in range(width):
        f, t, e = d // part, d % part // per, d % per
        at = ((e * (part // per) + t) * fold + f) * sequences
        for r in range(own_rows):
            out_ref[at : at + sequences, r * channels : (r + 1) * channels] = product[
                r * sequences : (r + 1) * sequences, d * channels : (d + 1) * channels
            ].astype(BF16)
    store.wait()


def pair_kernel(
    second_ref, right_ref, other_ref, spread_ref, pair_ref, weight_ref, gate_weight_ref,
    one_ref, gate_ref, out_ref,
    *, sequences,
):
    own_rows, columns, channels = pair_ref.shape
    first, second = ordered(
        second_ref[0], right_ref[...].astype(F32), other_ref[...].astype(F32)
    )
    right = [
        jnp.concatenate([first[:, e : e + own_rows], second[:, e : e + own_rows]], 1).reshape(
            columns, right_ref.shape[-1]
        )
        for e in range(0, right_ref.shape[1], own_rows)
    ]
    right = jnp.concatenate(right, 1).astype(BF16)
    update = dot(right, spread_ref[...]) * (1.0 / sequences)
    ones = [
        pair_ref[i].astype(F32) + update[:, i * channels : (i + 1) * channels]
        for i in range(own_rows)
    ]
    one = jnp.concatenate(ones, 0)
    one_ref[...] = one
    normed = normalized(one, -1).astype(BF16)
    gate_ref[...] = jax.nn.sigmoid(dot(normed, gate_weight_ref[...]))
    factors = dot_t(weight_ref[...], normed)
    left = jax.nn.sigmoid(factors[channels : 2 * channels]) * factors[:channels]
    right = jax.nn.sigmoid(factors[3 * channels :]) * factors[2 * channels : 3 * channels]
    both = jnp.concatenate([left.astype(BF16), right.astype(BF16)], 1)
    out_ref[...] = both.reshape(out_ref.shape)


def triangle_kernel(both_ref, out_ref, *, own_rows):
    devices, own_channels, lanes = both_ref.shape
    columns = lanes // 2 // own_rows
    size = devices * own_channels
    both = both_ref[...].reshape(size, lanes)
    left = jnp.concatenate([both[:, i * columns : (i + 1) * columns] for i in range(own_rows)], 0)
    right = jnp.concatenate(
        [both[:, (own_rows + i) * columns : (own_rows + i + 1) * columns] for i in range(own_rows)],
        0,
    )
    total = size * own_rows
    order = selector(
        total,
        lambda p: p % own_rows * size + p % columns // own_rows * own_channels + p // columns,
    )
    right = dot(order, right).astype(BF16)
    channel = iota((total, 1), 0) % own_channels
    combined = jnp.zeros((total, columns), F32)
    for c in range(own_channels):
        part = dot_t(left, right[c * columns : (c + 1) * columns])
        combined = jnp.where(channel == c, part, combined)
    combined = combined.astype(BF16)
    out_ref[...] = jnp.concatenate(
        [combined[i * size : (i + 1) * size] for i in range(own_rows)], 1
    ).reshape(out_ref.shape)


def final_kernel(back_ref, one_ref, gate_ref, weight_ref, out_ref):
    channels = weight_ref.shape[0]
    combined = back_ref[...].reshape(channels, back_ref.shape[-1]).astype(F32)
    normed = normalized(combined, 0).astype(BF16)
    update = t_dot(normed, weight_ref[...])
    out_ref[...] = (one_ref[...] + gate_ref[...] * update).astype(BF16).reshape(out_ref.shape)


def exchanged(x):
    return lax.all_to_all(x, "res", split_axis=0, concat_axis=0, tiled=True)


def shards(
    homolog_symbol_ids,
    residue_attend_mask,
    alignment_state,
    pair,
    symbol_lookup_matrix,
    pair_bias_weight,
    row_projection_weight,
    horizontal_readout_matrix,
    column_projection_weight,
    vertical_readout_matrix,
    product_factor_matrices,
    outer_output_weight,
    triangle_input_weight,
    triangle_output_weight,
):
    devices = lax.axis_size("res")
    own_sequences, length, channels = alignment_state.shape
    sequences = own_sequences * devices
    own_rows, columns, pair_channels = pair.shape
    heads = pair_bias_weight.shape[1]
    width = product_factor_matrices.shape[1] // 2
    own_channels = pair_channels // devices
    rows = own_sequences * length

    groups = [list(range(first, devices, 2)) for first in range(2)]
    half = devices // 2
    second = (lax.axis_index("res") % 2).reshape(1)

    def among_class(x):
        return lax.all_to_all(x, "res", 0, 0, axis_index_groups=groups, tiled=True)

    def from_other_core(x):
        return lax.ppermute(x, "res", [(i, i ^ 1) for i in range(devices)])

    (bias,) = kernel_call(
        bias_kernel,
        [((half, own_rows * heads, columns), BF16)],
        (pair, pair_bias_weight.T),
        "bias",
        fetched=(0, 1),
    )
    bias = among_class(bias)
    factors = product_factor_matrices.T
    scores, value, gate, start, readout, wide = kernel_call(
        functools.partial(row_scores_kernel, heads=heads, own_rows=own_rows),
        [
            ((2 * own_sequences, length // 2 * heads, length), F32),
            ((2 * rows, channels), BF16),
            ((rows, channels), F32),
            ((rows, channels), F32),
            ((channels, channels), BF16),
            ((width * own_rows, own_rows * channels), BF16),
        ],
        (
            second,
            homolog_symbol_ids,
            from_other_core(homolog_symbol_ids),
            residue_attend_mask.reshape(1, length),
            alignment_state,
            from_other_core(alignment_state),
            symbol_lookup_matrix,
            row_projection_weight,
            horizontal_readout_matrix,
            factors,
        ),
        "row_scores",
        flops=2 * rows * channels * 4 * channels,
        nbytes=1 << 21,
        scalars=1,
        fetched=(1, 3, 4, 6, 7, 8, 9),
    )
    (after_rows,) = kernel_call(
        functools.partial(row_mix_kernel, heads=heads),
        [((half, 2 * own_sequences * own_rows, channels), BF16)],
        (scores, bias, value, gate, start, readout),
        "row_mix",
    )
    by_residue = among_class(after_rows)
    per = max(1, 8 // own_rows)
    aligned, left, right = kernel_call(
        functools.partial(column_kernel, heads=heads, own_rows=own_rows),
        [
            ((sequences, own_rows, channels), BF16),
            ((sequences * own_rows, width), BF16),
            ((half, per * own_rows, width * sequences // per), BF16),
        ],
        (by_residue, column_projection_weight, vertical_readout_matrix, factors, wide),
        "column",
    )
    right = among_class(right)
    other = from_other_core(right)
    inside = pl.BlockSpec(memory_space=pltpu.VMEM)
    outside = pl.BlockSpec(memory_space=pl.ANY)
    spread, alignment_output = pl.pallas_call(
        functools.partial(spread_kernel, own_rows=own_rows, per=per),
        out_shape=(
            jax.ShapeDtypeStruct((width * sequences, own_rows * pair_channels), BF16),
            jax.ShapeDtypeStruct(aligned.shape, BF16),
        ),
        in_specs=[inside] * 3,
        out_specs=(inside, outside),
        scratch_shapes=[pltpu.SemaphoreType.DMA],
        compiler_params=pltpu.CompilerParams(vmem_limit_bytes=VMEM_BYTES),
        cost_estimate=pl.CostEstimate(
            flops=2 * own_rows * sequences * width * width * pair_channels,
            bytes_accessed=1 << 21,
            transcendentals=0,
        ),
        name="spread",
    )(aligned, left, outer_output_weight.reshape(width, width * pair_channels))
    pair_one, gate_out, both = kernel_call(
        functools.partial(pair_kernel, sequences=sequences),
        [
            ((own_rows * columns, pair_channels), F32),
            ((own_rows * columns, pair_channels), F32),
            ((devices, own_channels, 2 * own_rows * columns), BF16),
        ],
        (
            second,
            right,
            other,
            spread,
            pair,
            triangle_input_weight[:, : 4 * pair_channels].T,
            triangle_input_weight[:, 4 * pair_channels :],
        ),
        "pair",
        scalars=1,
    )
    both = exchanged(both)
    (combined,) = kernel_call(
        functools.partial(triangle_kernel, own_rows=own_rows),
        [((devices, own_channels, own_rows * columns), BF16)],
        (both,),
        "triangle",
    )
    back = exchanged(combined)
    (pair_output,) = kernel_call(
        final_kernel,
        [((own_rows, columns, pair_channels), BF16)],
        (back, pair_one, gate_out, triangle_output_weight),
        "final",
    )
    return (alignment_output, pair_output)


def solution(mesh):
    placed = (
        P(("crop", "res"), None),
        P("crop"),
        P(("crop", "res"), None, None),
        P(("crop", "res"), None, None),
    ) + (P(),) * 10
    return jax.shard_map(
        shards,
        mesh=mesh,
        in_specs=placed,
        out_specs=(P("crop", "res", None), P(("crop", "res"), None, None)),
        check_vma=False,
    )
```

```python
import functools

import jax
import jax.numpy as jnp
from jax import lax
from jax.experimental import pallas as pl
from jax.experimental.pallas import tpu as pltpu
from jax.sharding import PartitionSpec as P

EPSILON = 1e-05
F32 = jnp.float32
BF16 = jnp.bfloat16
VMEM_BYTES = 48 * 1024 * 1024


def normalized(rows, axis):
    average = jnp.mean(rows, axis, keepdims=True)
    centred = rows - average
    spread = jnp.mean(centred * centred, axis, keepdims=True)
    return centred * lax.rsqrt(spread + EPSILON)


def dot(a, b):
    return jnp.dot(a, b, preferred_element_type=F32)


def dot_t(a, b):
    return lax.dot_general(a, b, (((1,), (1,)), ((), ())), preferred_element_type=F32)


def t_dot(a, b):
    return lax.dot_general(a, b, (((0,), (0,)), ((), ())), preferred_element_type=F32)


def iota(shape, axis):
    return lax.broadcasted_iota(jnp.int32, shape, axis)


def selector(size, source_of):
    shape = (size, size)
    return (iota(shape, 1) == source_of(iota((size, 1), 0))).astype(F32).astype(BF16)


def swapped(outer, inner):
    return lambda p: (p % outer) * inner + p // outer


def lane_parts(channels, heads):
    lanes = min(128, channels)
    return [slice(at, at + lanes) for at in range(0, channels, lanes)], lanes * heads // channels


def own_channels_of(rows, lanes, width, first, own_rows):
    shape = (rows, lanes)
    return iota(shape, 0) // own_rows + first == iota(shape, 1) // width


def picked(pieces, masks):
    total = jnp.zeros_like(pieces[0])
    for piece, mask in zip(pieces, masks):
        total = jnp.where(jnp.broadcast_to(mask, piece.shape), piece, total)
    return total


def kernel_call(body, outs, args, name, flops=0, nbytes=0, scalars=0, fetched=()):
    inside = pl.BlockSpec(memory_space=pltpu.VMEM)
    outside = pl.BlockSpec(memory_space=pl.ANY)
    scalar = pl.BlockSpec(memory_space=pltpu.SMEM)
    args = [
        pltpu.with_memory_space_constraint(a, pltpu.HBM) if i in fetched else a
        for i, a in enumerate(args)
    ]

    def fetching(*refs):
        refs, held, sems = list(refs[: len(args) + len(outs)]), refs[len(args) + len(outs) : -1], refs[-1]
        copies = []
        for k, i in enumerate(fetched):
            copies.append(pltpu.make_async_copy(refs[i], held[k], sems.at[k]))
            copies[-1].start()
            refs[i] = held[k]
        for copy in copies:
            copy.wait()
        body(*refs)

    scratch = [pltpu.VMEM(args[i].shape, args[i].dtype) for i in fetched]
    return pl.pallas_call(
        fetching if fetched else body,
        out_shape=tuple(jax.ShapeDtypeStruct(s, d) for s, d in outs),
        in_specs=[
            scalar if i < scalars else outside if i in fetched else inside
            for i in range(len(args))
        ],
        out_specs=(inside,) * len(outs),
        scratch_shapes=scratch + [pltpu.SemaphoreType.DMA((len(fetched),))] if fetched else [],
        compiler_params=pltpu.CompilerParams(vmem_limit_bytes=VMEM_BYTES),
        cost_estimate=pl.CostEstimate(flops=flops, bytes_accessed=nbytes, transcendentals=0),
        name=name,
    )(*args)


def bias_kernel(pair_ref, weight_ref, out_ref):
    rows, columns, channels = pair_ref.shape
    x = pair_ref[...].reshape(rows * columns, channels).astype(F32)
    normed = normalized(x, -1).astype(BF16)
    weight = weight_ref[...].astype(F32)
    heads = weight.shape[0]
    weight = jnp.broadcast_to(weight[:, None, :], (heads, rows, channels))
    weight = weight.reshape(heads * rows, channels).astype(BF16)
    bias = dot_t(weight, normed)
    row = iota((heads * rows, columns), 0) % rows
    block = bias[:, :columns]
    for i in range(1, rows):
        block = jnp.where(row == i, bias[:, i * columns : (i + 1) * columns], block)
    block = block.astype(BF16)
    for d in range(out_ref.shape[0]):
        out_ref[d] = block


def ordered(second, mine, other):
    flip = jnp.full(mine.shape, second, jnp.int32) == 1
    return jnp.where(flip, other, mine), jnp.where(flip, mine, other)


def row_scores_kernel(
    second_ref, ids_ref, other_ids_ref, mask_ref, state_ref, other_ref, table_ref, weight_ref,
    readout_ref, factor_ref,
    scores_ref, value_ref, gate_ref, start_ref, held_ref, wide_ref,
    *, heads, own_rows,
):
    own_sequences, length, channels = state_ref.shape
    tokens = table_ref.shape[0]
    second = second_ref[0]
    held_ref[...] = readout_ref[...]
    ids = jnp.concatenate(ordered(second, ids_ref[...], other_ids_ref[...]), 0)
    states = jnp.concatenate(
        ordered(second, state_ref[...].astype(F32), other_ref[...].astype(F32)), 0
    )
    sequences = 2 * own_sequences
    starts = []
    for s in range(sequences):
        hot = (iota((tokens, length), 0) == ids[s : s + 1, :]).astype(F32).astype(BF16)
        starts.append(states[s] + t_dot(hot, table_ref[...]))
    start = jnp.concatenate(starts, 0)
    normed = normalized(start, -1)
    projected = dot(normed.astype(BF16), weight_ref[:, channels : 3 * channels])
    key = projected[:, :channels].astype(BF16)
    value_ref[...] = projected[:, channels:].astype(BF16)

    def mine(x):
        pairs = x.reshape(sequences * length // (2 * own_rows), 2 * own_rows, channels)
        low, high = pairs[:, :own_rows], pairs[:, own_rows:]
        return ordered(second, low, high)[0].reshape(sequences * length // 2, channels)

    start_ref[...] = mine(start)
    own = mine(normed)
    per = max(1, 8 // own_rows)
    own = own.reshape(own.shape[0] // own_rows, own_rows, channels)
    own = jnp.concatenate([own] * per, 1).reshape(-1, channels).astype(BF16)
    query = dot(own, weight_ref[:, :channels]) * (channels // heads) ** (-0.5)
    query = query.astype(BF16).astype(F32)
    gate_ref[...] = jax.nn.sigmoid(dot(own, weight_ref[:, 3 * channels :]))
    extra = (mask_ref[...].astype(F32) - 1.0) * 10000.0
    tall = query.shape[0] // sequences
    block = per * own_rows
    parts, inner = lane_parts(channels, heads)
    masks = [
        own_channels_of(block, channels // len(parts), channels // heads, h, own_rows)[None]
        for h in range(0, inner, per)
    ]
    size = len(masks) * tall
    for s in range(sequences):
        for u, part in enumerate(parts):
            rows = query[s * tall : (s + 1) * tall, part]
            rows = rows.reshape(tall // block, block, rows.shape[1])
            spread = [
                picked([rows], [mask]).reshape(tall, rows.shape[2]).astype(BF16) for mask in masks
            ]
            scores_ref[s, u * size : (u + 1) * size] = (
                dot_t(jnp.concatenate(spread, 0), key[s * length : (s + 1) * length, part]) + extra
            )
    width = factor_ref.shape[0] // 2
    right = factor_ref[width:].astype(F32)
    repeated = jnp.broadcast_to(right[:, None, :], (width, own_rows, channels)).reshape(
        width * own_rows, channels
    )
    row = iota(repeated.shape, 0) % own_rows
    for r in range(own_rows):
        wide_ref[:, r * channels : (r + 1) * channels] = jnp.where(row == r, repeated, 0.0).astype(
            BF16
        )


def softmax_parts(scores):
    e = jnp.exp(scores - jnp.max(scores, -1, keepdims=True))
    return e.astype(BF16), 1.0 / jnp.sum(e, -1, keepdims=True)


def row_mix_kernel(
    scores_ref, bias_ref, value_ref, gate_ref, start_ref, weight_ref, out_ref, *, heads, own_rows
):
    sequences, expanded, length = scores_ref.shape
    channels = value_ref.shape[1]
    groups = out_ref.shape[0]
    per = max(1, 8 // own_rows)
    tiles = heads // per
    block = per * own_rows
    tall = groups * block
    bias = bias_ref[...].astype(F32)
    bias = jnp.concatenate(
        [
            bias[:, t * block : (t + 1) * block].reshape(tall, length)
            for t in range(tiles)
        ],
        0,
    )
    parts, inner = lane_parts(channels, heads)
    masks = [
        own_channels_of(block, channels // len(parts), channels // heads, h, own_rows)[None]
        for h in range(0, inner, per)
    ]
    size = len(masks) * tall
    pieces = []
    for s in range(sequences):
        weights, scale = softmax_parts(scores_ref[s] + bias)
        mixed = []
        for u, part in enumerate(parts):
            rows = slice(u * size, (u + 1) * size)
            whole = dot(weights[rows], value_ref[s * length : (s + 1) * length, part])
            whole = whole * scale[rows]
            whole = whole.reshape(len(masks), groups, block, whole.shape[1])
            mixed.append(
                picked([whole[t] for t in range(len(masks))], masks).reshape(tall, whole.shape[3])
            )
        mixed = jnp.concatenate(mixed, 1)
        gated = (gate_ref[s * tall : (s + 1) * tall] * mixed).astype(BF16)
        update = dot(gated, weight_ref[...]).reshape(groups, block, channels)
        after = start_ref[s * groups * own_rows : (s + 1) * groups * own_rows].reshape(
            groups, own_rows, channels
        )
        for h in range(per):
            after = after + update[:, h * own_rows : (h + 1) * own_rows]
        pieces.append(after)
    out_ref[...] = jnp.concatenate(pieces, 1).astype(BF16)


def column_kernel(
    state_ref, weight_ref, readout_ref, factor_ref, wide_ref, out_ref, left_ref, right_ref,
    *, heads, own_rows,
):
    devices, block, channels = state_ref.shape
    size = devices * block
    sequences = size // own_rows
    to_rows = selector(size, swapped(sequences, own_rows))
    to_sequences = selector(size, swapped(own_rows, sequences))
    start = dot(to_rows, state_ref[...].reshape(size, channels))
    projected = dot(normalized(start, -1).astype(BF16), weight_ref[...])
    query = (projected[:, :channels] * (channels // heads) ** (-0.5)).astype(BF16).astype(F32)
    key = projected[:, channels : 2 * channels].astype(BF16)
    value = projected[:, 2 * channels : 3 * channels].astype(BF16)
    gate = jax.nn.sigmoid(projected[:, 3 * channels :])
    parts, inner = lane_parts(channels, heads)
    masks = [
        own_channels_of(1, channels // len(parts), channels // heads, h, 1) for h in range(inner)
    ]
    gated = []
    for r in range(own_rows):
        rows = slice(r * sequences, (r + 1) * sequences)
        mixed = []
        for part in parts:
            spread = [picked([query[rows, part]], [mask]).astype(BF16) for mask in masks]
            weights, scale = softmax_parts(dot_t(jnp.concatenate(spread, 0), key[rows, part]))
            whole = dot(weights, value[rows, part]) * scale
            mixed.append(
                picked(
                    [whole[h * sequences : (h + 1) * sequences] for h in range(inner)], masks
                )
            )
        gated.append((gate[rows] * jnp.concatenate(mixed, 1)).astype(BF16))
    after = start + dot(jnp.concatenate(gated, 0), readout_ref[...])
    normed = normalized(after, -1).astype(BF16)
    width = factor_ref.shape[0] // 2
    fold = max(1, 128 // sequences)
    part = width // fold
    side = jnp.concatenate(
        [normed[r * sequences : (r + 1) * sequences] for r in range(own_rows)], 1
    )
    right = dot_t(wide_ref[...], side)
    cut = part * own_rows
    right = jnp.concatenate([right[f * cut : (f + 1) * cut] for f in range(fold)], 1)
    tall = right_ref.shape[1]
    packed = jnp.concatenate(
        [right[t * tall : (t + 1) * tall] for t in range(cut // tall)], 1
    ).astype(BF16)
    for d in range(right_ref.shape[0]):
        right_ref[d] = packed
    left_ref[...] = dot_t(normed, factor_ref[:width]).astype(BF16)
    out_ref[...] = dot(to_sequences, after.astype(BF16)).astype(BF16).reshape(out_ref.shape)


def half_update(right, spread, own_rows):
    groups, tall, lanes = right.shape
    columns = spread.shape[1] * own_rows // tall
    whole = dot(right.reshape(groups * tall, lanes), spread).reshape(groups, tall, -1)
    total = whole[:, :own_rows, :columns]
    for e in range(1, tall // own_rows):
        total = total + whole[
            :, e * own_rows : (e + 1) * own_rows, e * columns : (e + 1) * columns
        ]
    return total


def spread_kernel(
    aligned_ref, right_ref, left_ref, weight_ref, out_ref, half_ref, final_ref, sem,
    *, own_rows, per,
):
    store = pltpu.make_async_copy(aligned_ref, final_ref, sem)
    store.start()
    size, width = left_ref.shape
    sequences = size // own_rows
    channels = weight_ref.shape[1] // width
    fold = max(1, 128 // sequences)
    part = width // fold
    product = dot(left_ref[...], weight_ref[...])
    for d in range(width):
        f, t, e = d // part, d % part // per, d % per
        at = (t * fold + f) * sequences
        for r in range(own_rows):
            to = (e * own_rows + r) * channels
            out_ref[at : at + sequences, to : to + channels] = product[
                r * sequences : (r + 1) * sequences, d * channels : (d + 1) * channels
            ].astype(BF16)
    half_ref[...] = half_update(right_ref[...], out_ref[...], own_rows)
    store.wait()


def pair_kernel(
    second_ref, half_ref, other_ref, spread_ref, pair_ref, weight_ref, gate_weight_ref,
    one_ref, gate_ref, out_ref,
    *, sequences,
):
    own_rows, columns, channels = pair_ref.shape
    halves = ordered(
        second_ref[0], half_ref[...], half_update(other_ref[...], spread_ref[...], own_rows)
    )
    update = jnp.concatenate(halves, 1).reshape(columns, own_rows * channels) * (1.0 / sequences)
    ones = [
        pair_ref[i].astype(F32) + update[:, i * channels : (i + 1) * channels]
        for i in range(own_rows)
    ]
    one = jnp.concatenate(ones, 0)
    one_ref[...] = one
    normed = normalized(one, -1).astype(BF16)
    gate_ref[...] = jax.nn.sigmoid(dot(normed, gate_weight_ref[...]))
    factors = dot_t(weight_ref[...], normed)
    left = jax.nn.sigmoid(factors[channels : 2 * channels]) * factors[:channels]
    right = jax.nn.sigmoid(factors[3 * channels :]) * factors[2 * channels : 3 * channels]
    both = jnp.concatenate([left.astype(BF16), right.astype(BF16)], 1)
    out_ref[...] = both.reshape(out_ref.shape)


def triangle_kernel(both_ref, out_ref, *, own_rows):
    devices, own_channels, lanes = both_ref.shape
    columns = lanes // 2 // own_rows
    size = devices * own_channels
    both = both_ref[...].reshape(size, lanes)
    left = jnp.concatenate([both[:, i * columns : (i + 1) * columns] for i in range(own_rows)], 0)
    right = jnp.concatenate(
        [both[:, (own_rows + i) * columns : (own_rows + i + 1) * columns] for i in range(own_rows)],
        0,
    )
    total = size * own_rows
    order = selector(
        total,
        lambda p: p % own_rows * size + p % columns // own_rows * own_channels + p // columns,
    )
    right = dot(order, right).astype(BF16)
    channel = iota((total, 1), 0) % own_channels
    combined = jnp.zeros((total, columns), F32)
    for c in range(own_channels):
        part = dot_t(left, right[c * columns : (c + 1) * columns])
        combined = jnp.where(channel == c, part, combined)
    combined = combined.astype(BF16)
    out_ref[...] = jnp.concatenate(
        [combined[i * size : (i + 1) * size] for i in range(own_rows)], 1
    ).reshape(out_ref.shape)


def final_kernel(back_ref, one_ref, gate_ref, weight_ref, out_ref):
    channels = weight_ref.shape[0]
    combined = back_ref[...].reshape(channels, back_ref.shape[-1]).astype(F32)
    normed = normalized(combined, 0).astype(BF16)
    update = t_dot(normed, weight_ref[...])
    out_ref[...] = (one_ref[...] + gate_ref[...] * update).astype(BF16).reshape(out_ref.shape)


def exchanged(x):
    return lax.all_to_all(x, "res", split_axis=0, concat_axis=0, tiled=True)


def shards(
    homolog_symbol_ids,
    residue_attend_mask,
    alignment_state,
    pair,
    symbol_lookup_matrix,
    pair_bias_weight,
    row_projection_weight,
    horizontal_readout_matrix,
    column_projection_weight,
    vertical_readout_matrix,
    product_factor_matrices,
    outer_output_weight,
    triangle_input_weight,
    triangle_output_weight,
):
    devices = lax.axis_size("res")
    own_sequences, length, channels = alignment_state.shape
    sequences = own_sequences * devices
    own_rows, columns, pair_channels = pair.shape
    heads = pair_bias_weight.shape[1]
    width = product_factor_matrices.shape[1] // 2
    own_channels = pair_channels // devices
    rows = own_sequences * length

    groups = [list(range(first, devices, 2)) for first in range(2)]
    half = devices // 2
    second = (lax.axis_index("res") % 2).reshape(1)

    def among_class(x):
        return lax.all_to_all(x, "res", 0, 0, axis_index_groups=groups, tiled=True)

    def from_other_core(x):
        return lax.ppermute(x, "res", [(i, i ^ 1) for i in range(devices)])

    (bias,) = kernel_call(
        bias_kernel,
        [((half, own_rows * heads, columns), BF16)],
        (pair, pair_bias_weight.T),
        "bias",
        fetched=(0, 1),
    )
    bias = among_class(bias)
    factors = product_factor_matrices.T
    scores, value, gate, start, readout, wide = kernel_call(
        functools.partial(row_scores_kernel, heads=heads, own_rows=own_rows),
        [
            ((2 * own_sequences, length // 2 * heads, length), F32),
            ((2 * rows, channels), BF16),
            ((rows * max(1, 8 // own_rows), channels), F32),
            ((rows, channels), F32),
            ((channels, channels), BF16),
            ((width * own_rows, own_rows * channels), BF16),
        ],
        (
            second,
            homolog_symbol_ids,
            from_other_core(homolog_symbol_ids),
            residue_attend_mask.reshape(1, length),
            alignment_state,
            from_other_core(alignment_state),
            symbol_lookup_matrix,
            row_projection_weight,
            horizontal_readout_matrix,
            factors,
        ),
        "row_scores",
        flops=2 * rows * channels * 4 * channels,
        nbytes=1 << 21,
        scalars=1,
        fetched=(1, 3, 4, 6, 7, 8, 9),
    )
    (after_rows,) = kernel_call(
        functools.partial(row_mix_kernel, heads=heads, own_rows=own_rows),
        [((half, 2 * own_sequences * own_rows, channels), BF16)],
        (scores, bias, value, gate, start, readout),
        "row_mix",
    )
    by_residue = among_class(after_rows)
    per = max(1, 8 // own_rows)
    aligned, left, right = kernel_call(
        functools.partial(column_kernel, heads=heads, own_rows=own_rows),
        [
            ((sequences, own_rows, channels), BF16),
            ((sequences * own_rows, width), BF16),
            ((half, per * own_rows, width * sequences // per), BF16),
        ],
        (by_residue, column_projection_weight, vertical_readout_matrix, factors, wide),
        "column",
    )
    right = among_class(right)
    other = from_other_core(right)
    inside = pl.BlockSpec(memory_space=pltpu.VMEM)
    outside = pl.BlockSpec(memory_space=pl.ANY)
    spread, update, alignment_output = pl.pallas_call(
        functools.partial(spread_kernel, own_rows=own_rows, per=per),
        out_shape=(
            jax.ShapeDtypeStruct(
                (width * sequences // per, per * own_rows * pair_channels), BF16
            ),
            jax.ShapeDtypeStruct((half, own_rows, own_rows * pair_channels), F32),
            jax.ShapeDtypeStruct(aligned.shape, BF16),
        ),
        in_specs=[inside] * 4,
        out_specs=(inside, inside, outside),
        scratch_shapes=[pltpu.SemaphoreType.DMA],
        compiler_params=pltpu.CompilerParams(vmem_limit_bytes=VMEM_BYTES),
        cost_estimate=pl.CostEstimate(
            flops=2 * own_rows * sequences * width * width * pair_channels,
            bytes_accessed=1 << 21,
            transcendentals=0,
        ),
        name="spread",
    )(aligned, right, left, outer_output_weight.reshape(width, width * pair_channels))
    pair_one, gate_out, both = kernel_call(
        functools.partial(pair_kernel, sequences=sequences),
        [
            ((own_rows * columns, pair_channels), F32),
            ((own_rows * columns, pair_channels), F32),
            ((devices, own_channels, 2 * own_rows * columns), BF16),
        ],
        (
            second,
            update,
            other,
            spread,
            pair,
            triangle_input_weight[:, : 4 * pair_channels].T,
            triangle_input_weight[:, 4 * pair_channels :],
        ),
        "pair",
        scalars=1,
    )
    both = exchanged(both)
    (combined,) = kernel_call(
        functools.partial(triangle_kernel, own_rows=own_rows),
        [((devices, own_channels, own_rows * columns), BF16)],
        (both,),
        "triangle",
    )
    back = exchanged(combined)
    (pair_output,) = kernel_call(
        final_kernel,
        [((own_rows, columns, pair_channels), BF16)],
        (back, pair_one, gate_out, triangle_output_weight),
        "final",
    )
    return (alignment_output, pair_output)


def solution(mesh):
    placed = (
        P(("crop", "res"), None),
        P("crop"),
        P(("crop", "res"), None, None),
        P(("crop", "res"), None, None),
    ) + (P(),) * 10
    return jax.shard_map(
        shards,
        mesh=mesh,
        in_specs=placed,
        out_specs=(P("crop", "res", None), P(("crop", "res"), None, None)),
        check_vma=False,
    )
```

```python
import functools

import jax
import jax.numpy as jnp
from jax import lax
from jax.experimental import pallas as pl
from jax.experimental.pallas import tpu as pltpu
from jax.sharding import PartitionSpec as P

EPSILON = 1e-05
F32 = jnp.float32
BF16 = jnp.bfloat16
VMEM_BYTES = 48 * 1024 * 1024


def normalized(rows, axis):
    average = jnp.mean(rows, axis, keepdims=True)
    centred = rows - average
    spread = jnp.mean(centred * centred, axis, keepdims=True)
    return centred * lax.rsqrt(spread + EPSILON)


def dot(a, b):
    return jnp.dot(a, b, preferred_element_type=F32)


def dot_t(a, b):
    return lax.dot_general(a, b, (((1,), (1,)), ((), ())), preferred_element_type=F32)


def t_dot(a, b):
    return lax.dot_general(a, b, (((0,), (0,)), ((), ())), preferred_element_type=F32)


def iota(shape, axis):
    return lax.broadcasted_iota(jnp.int32, shape, axis)


def selector(size, source_of):
    shape = (size, size)
    return (iota(shape, 1) == source_of(iota((size, 1), 0))).astype(F32).astype(BF16)


def swapped(outer, inner):
    return lambda p: (p % outer) * inner + p // outer


def lane_parts(channels, heads):
    lanes = min(128, channels)
    return [slice(at, at + lanes) for at in range(0, channels, lanes)], lanes * heads // channels


def own_channels_of(rows, lanes, width, first, own_rows):
    shape = (rows, lanes)
    return iota(shape, 0) // own_rows + first == iota(shape, 1) // width


def picked(pieces, masks):
    total = jnp.zeros_like(pieces[0])
    for piece, mask in zip(pieces, masks):
        total = jnp.where(jnp.broadcast_to(mask, piece.shape), piece, total)
    return total


def kernel_call(body, outs, args, name, flops=0, nbytes=0, scalars=0, fetched=(), scratch=()):
    inside = pl.BlockSpec(memory_space=pltpu.VMEM)
    outside = pl.BlockSpec(memory_space=pl.ANY)
    scalar = pl.BlockSpec(memory_space=pltpu.SMEM)
    args = [
        pltpu.with_memory_space_constraint(a, pltpu.HBM) if i in fetched else a
        for i, a in enumerate(args)
    ]

    def fetching(*refs):
        refs, held, sems = list(refs[: len(args) + len(outs)]), refs[len(args) + len(outs) : -1], refs[-1]
        copies = []
        for k, i in enumerate(fetched):
            copies.append(pltpu.make_async_copy(refs[i], held[k], sems.at[k]))
            copies[-1].start()
            refs[i] = held[k]
        for copy in copies:
            copy.wait()
        body(*refs)

    held = [pltpu.VMEM(args[i].shape, args[i].dtype) for i in fetched]
    if fetched:
        held.append(pltpu.SemaphoreType.DMA((len(fetched),)))
    return pl.pallas_call(
        fetching if fetched else body,
        out_shape=tuple(jax.ShapeDtypeStruct(s, d) for s, d in outs),
        in_specs=[
            scalar if i < scalars else outside if i in fetched else inside
            for i in range(len(args))
        ],
        out_specs=(inside,) * len(outs),
        scratch_shapes=held + list(scratch),
        compiler_params=pltpu.CompilerParams(vmem_limit_bytes=VMEM_BYTES),
        cost_estimate=pl.CostEstimate(flops=flops, bytes_accessed=nbytes, transcendentals=0),
        name=name,
    )(*args)


def bias_kernel(pair_ref, weight_ref, out_ref):
    rows, columns, channels = pair_ref.shape
    x = pair_ref[...].reshape(rows * columns, channels).astype(F32)
    normed = normalized(x, -1).astype(BF16)
    weight = weight_ref[...].astype(F32)
    heads = weight.shape[0]
    weight = jnp.broadcast_to(weight[:, None, :], (heads, rows, channels))
    weight = weight.reshape(heads * rows, channels).astype(BF16)
    bias = dot_t(weight, normed)
    row = iota((heads * rows, columns), 0) % rows
    block = bias[:, :columns]
    for i in range(1, rows):
        block = jnp.where(row == i, bias[:, i * columns : (i + 1) * columns], block)
    block = block.astype(BF16)
    for d in range(out_ref.shape[0]):
        out_ref[d] = block


def ordered(second, mine, other):
    flip = jnp.full(mine.shape, second, jnp.int32) == 1
    return jnp.where(flip, other, mine), jnp.where(flip, mine, other)


def row_scores_kernel(
    second_ref, ids_ref, other_ids_ref, mask_ref, state_ref, other_ref, table_ref, weight_ref,
    readout_ref, factor_ref,
    scores_ref, value_ref, gate_ref, start_ref, held_ref, wide_ref,
    *, heads, own_rows,
):
    own_sequences, length, channels = state_ref.shape
    tokens = table_ref.shape[0]
    second = second_ref[0]
    held_ref[...] = readout_ref[...]
    ids = jnp.concatenate(ordered(second, ids_ref[...], other_ids_ref[...]), 0)
    states = jnp.concatenate(
        ordered(second, state_ref[...].astype(F32), other_ref[...].astype(F32)), 0
    )
    sequences = 2 * own_sequences
    starts = []
    for s in range(sequences):
        hot = (iota((tokens, length), 0) == ids[s : s + 1, :]).astype(F32).astype(BF16)
        starts.append(states[s] + t_dot(hot, table_ref[...]))
    start = jnp.concatenate(starts, 0)
    normed = normalized(start, -1)
    projected = dot(normed.astype(BF16), weight_ref[:, channels : 3 * channels])
    key = projected[:, :channels].astype(BF16)
    value_ref[...] = projected[:, channels:].astype(BF16)

    def mine(x):
        pairs = x.reshape(sequences * length // (2 * own_rows), 2 * own_rows, channels)
        low, high = pairs[:, :own_rows], pairs[:, own_rows:]
        return ordered(second, low, high)[0].reshape(sequences * length // 2, channels)

    start_ref[...] = mine(start)
    own = mine(normed)
    per = max(1, 8 // own_rows)
    own = own.reshape(own.shape[0] // own_rows, own_rows, channels)
    own = jnp.concatenate([own] * per, 1).reshape(-1, channels).astype(BF16)
    query = dot(own, weight_ref[:, :channels]) * (channels // heads) ** (-0.5)
    query = query.astype(BF16).astype(F32)
    gate_ref[...] = jax.nn.sigmoid(dot(own, weight_ref[:, 3 * channels :]))
    extra = (mask_ref[...].astype(F32) - 1.0) * 10000.0
    tall = query.shape[0] // sequences
    block = per * own_rows
    parts, inner = lane_parts(channels, heads)
    masks = [
        own_channels_of(block, channels // len(parts), channels // heads, h, own_rows)[None]
        for h in range(0, inner, per)
    ]
    size = len(masks) * tall
    for s in range(sequences):
        for u, part in enumerate(parts):
            rows = query[s * tall : (s + 1) * tall, part]
            rows = rows.reshape(tall // block, block, rows.shape[1])
            spread = [
                picked([rows], [mask]).reshape(tall, rows.shape[2]).astype(BF16) for mask in masks
            ]
            scores_ref[s, u * size : (u + 1) * size] = (
                dot_t(jnp.concatenate(spread, 0), key[s * length : (s + 1) * length, part]) + extra
            )
    width = factor_ref.shape[0] // 2
    right = factor_ref[width:].astype(F32)
    repeated = jnp.broadcast_to(right[:, None, :], (width, own_rows, channels)).reshape(
        width * own_rows, channels
    )
    row = iota(repeated.shape, 0) % own_rows
    for r in range(own_rows):
        wide_ref[:, r * channels : (r + 1) * channels] = jnp.where(row == r, repeated, 0.0).astype(
            BF16
        )


def softmax_parts(scores):
    e = jnp.exp(scores - jnp.max(scores, -1, keepdims=True))
    return e.astype(BF16), 1.0 / jnp.sum(e, -1, keepdims=True)


def row_mix_kernel(
    scores_ref, bias_ref, value_ref, gate_ref, start_ref, weight_ref, out_ref, *, heads, own_rows
):
    sequences, expanded, length = scores_ref.shape
    channels = value_ref.shape[1]
    groups = out_ref.shape[0]
    per = max(1, 8 // own_rows)
    tiles = heads // per
    block = per * own_rows
    tall = groups * block
    bias = bias_ref[...].astype(F32)
    bias = jnp.concatenate(
        [
            bias[:, t * block : (t + 1) * block].reshape(tall, length)
            for t in range(tiles)
        ],
        0,
    )
    parts, inner = lane_parts(channels, heads)
    masks = [
        own_channels_of(block, channels // len(parts), channels // heads, h, own_rows)[None]
        for h in range(0, inner, per)
    ]
    size = len(masks) * tall
    pieces = []
    for s in range(sequences):
        weights, scale = softmax_parts(scores_ref[s] + bias)
        mixed = []
        for u, part in enumerate(parts):
            rows = slice(u * size, (u + 1) * size)
            whole = dot(weights[rows], value_ref[s * length : (s + 1) * length, part])
            whole = whole * scale[rows]
            whole = whole.reshape(len(masks), groups, block, whole.shape[1])
            mixed.append(
                picked([whole[t] for t in range(len(masks))], masks).reshape(tall, whole.shape[3])
            )
        mixed = jnp.concatenate(mixed, 1)
        gated = (gate_ref[s * tall : (s + 1) * tall] * mixed).astype(BF16)
        update = dot(gated, weight_ref[...]).reshape(groups, block, channels)
        after = start_ref[s * groups * own_rows : (s + 1) * groups * own_rows].reshape(
            groups, own_rows, channels
        )
        for h in range(per):
            after = after + update[:, h * own_rows : (h + 1) * own_rows]
        pieces.append(after)
    out_ref[...] = jnp.concatenate(pieces, 1).astype(BF16)


def column_kernel(
    state_ref, weight_ref, readout_ref, factor_ref, wide_ref, out_ref, left_ref, right_ref,
    *, heads, own_rows,
):
    devices, block, channels = state_ref.shape
    size = devices * block
    sequences = size // own_rows
    to_rows = selector(size, swapped(sequences, own_rows))
    to_sequences = selector(size, swapped(own_rows, sequences))
    start = dot(to_rows, state_ref[...].reshape(size, channels))
    projected = dot(normalized(start, -1).astype(BF16), weight_ref[...])
    query = (projected[:, :channels] * (channels // heads) ** (-0.5)).astype(BF16).astype(F32)
    key = projected[:, channels : 2 * channels].astype(BF16)
    value = projected[:, 2 * channels : 3 * channels].astype(BF16)
    gate = jax.nn.sigmoid(projected[:, 3 * channels :])
    parts, inner = lane_parts(channels, heads)
    masks = [
        own_channels_of(1, channels // len(parts), channels // heads, h, 1) for h in range(inner)
    ]
    gated = []
    for r in range(own_rows):
        rows = slice(r * sequences, (r + 1) * sequences)
        mixed = []
        for part in parts:
            spread = [picked([query[rows, part]], [mask]).astype(BF16) for mask in masks]
            weights, scale = softmax_parts(dot_t(jnp.concatenate(spread, 0), key[rows, part]))
            whole = dot(weights, value[rows, part]) * scale
            mixed.append(
                picked(
                    [whole[h * sequences : (h + 1) * sequences] for h in range(inner)], masks
                )
            )
        gated.append((gate[rows] * jnp.concatenate(mixed, 1)).astype(BF16))
    after = start + dot(jnp.concatenate(gated, 0), readout_ref[...])
    normed = normalized(after, -1).astype(BF16)
    width = factor_ref.shape[0] // 2
    fold = max(1, 128 // sequences)
    part = width // fold
    side = jnp.concatenate(
        [normed[r * sequences : (r + 1) * sequences] for r in range(own_rows)], 1
    )
    right = dot_t(wide_ref[...], side)
    cut = part * own_rows
    right = jnp.concatenate([right[f * cut : (f + 1) * cut] for f in range(fold)], 1)
    tall = right_ref.shape[1]
    packed = jnp.concatenate(
        [right[t * tall : (t + 1) * tall] for t in range(cut // tall)], 1
    ).astype(BF16)
    for d in range(right_ref.shape[0]):
        right_ref[d] = packed
    left_ref[...] = dot_t(normed, factor_ref[:width]).astype(BF16)
    out_ref[...] = dot(to_sequences, after.astype(BF16)).astype(BF16).reshape(out_ref.shape)


def half_update(right, spread, own_rows):
    groups, tall, lanes = right.shape
    columns = spread.shape[1] * own_rows // tall
    whole = dot(right.reshape(groups * tall, lanes), spread).reshape(groups, tall, -1)
    total = whole[:, :own_rows, :columns]
    for e in range(1, tall // own_rows):
        total = total + whole[
            :, e * own_rows : (e + 1) * own_rows, e * columns : (e + 1) * columns
        ]
    return total


def spread_kernel(
    aligned_ref, right_ref, left_ref, weight_ref, out_ref, half_ref, final_ref, sem,
    *, own_rows, per,
):
    store = pltpu.make_async_copy(aligned_ref, final_ref, sem)
    store.start()
    size, width = left_ref.shape
    sequences = size // own_rows
    channels = weight_ref.shape[1] // width
    fold = max(1, 128 // sequences)
    part = width // fold
    product = dot(left_ref[...], weight_ref[...])
    for d in range(width):
        f, t, e = d // part, d % part // per, d % per
        at = (t * fold + f) * sequences
        for r in range(own_rows):
            to = (e * own_rows + r) * channels
            out_ref[at : at + sequences, to : to + channels] = product[
                r * sequences : (r + 1) * sequences, d * channels : (d + 1) * channels
            ].astype(BF16)
    half_ref[...] = half_update(right_ref[...], out_ref[...], own_rows)
    store.wait()


def pair_kernel(
    second_ref, half_ref, other_ref, spread_ref, pair_ref, weight_ref, gate_weight_ref,
    one_ref, gate_ref, out_ref,
    *, sequences,
):
    own_rows, columns, channels = pair_ref.shape
    halves = ordered(
        second_ref[0], half_ref[...], half_update(other_ref[...], spread_ref[...], own_rows)
    )
    update = jnp.concatenate(halves, 1).reshape(columns, own_rows * channels) * (1.0 / sequences)
    ones = [
        pair_ref[i].astype(F32) + update[:, i * channels : (i + 1) * channels]
        for i in range(own_rows)
    ]
    one = jnp.concatenate(ones, 0)
    one_ref[...] = one
    normed = normalized(one, -1).astype(BF16)
    gate_ref[...] = jax.nn.sigmoid(dot(normed, gate_weight_ref[...]))
    factors = dot_t(weight_ref[...], normed)
    left = jax.nn.sigmoid(factors[channels : 2 * channels]) * factors[:channels]
    right = jax.nn.sigmoid(factors[3 * channels :]) * factors[2 * channels : 3 * channels]
    both = jnp.concatenate([left.astype(BF16), right.astype(BF16)], 1)
    out_ref[...] = both.reshape(out_ref.shape)


def triangle_kernel(both_ref, out_ref, left_ref, right_ref, ordered_ref, *, own_rows):
    devices, own_channels, lanes = both_ref.shape
    columns = lanes // 2 // own_rows
    size = devices * own_channels
    tile = left_ref.shape[2]
    tiles = columns // tile
    both = both_ref[...].reshape(size, lanes).astype(F32)
    for i in range(own_rows):
        rows = slice(i * size, (i + 1) * size)
        for k in range(tiles):
            at = i * columns + k * tile
            left_ref[k, rows] = both[:, at : at + tile]
            at += own_rows * columns
            right_ref[k, rows] = both[:, at : at + tile]

    def channel_rows(c, i):
        return pl.ds(i * size + c, devices, stride=own_channels)

    for k in range(tiles):
        for c in range(own_channels):
            for i in range(own_rows):
                ordered_ref[k, pl.ds(c * columns + i, devices, stride=own_rows), :] = right_ref[
                    k, channel_rows(c, i), :
                ]
    for c in range(own_channels):
        combined = jnp.zeros((columns, columns), F32)
        for k in range(tiles):
            left = jnp.concatenate(
                [left_ref[k, channel_rows(c, i), :] for i in range(own_rows)], 0
            )
            right = ordered_ref[k, c * columns : (c + 1) * columns]
            combined = combined + dot_t(left.astype(BF16), right.astype(BF16))
        for i in range(own_rows):
            for k in range(tiles):
                right_ref[k, channel_rows(c, i), :] = combined[
                    i * devices : (i + 1) * devices, k * tile : (k + 1) * tile
                ]
    out_ref[...] = (
        jnp.concatenate(
            [
                right_ref[k, i * size : (i + 1) * size]
                for i in range(own_rows)
                for k in range(tiles)
            ],
            1,
        )
        .astype(BF16)
        .reshape(out_ref.shape)
    )


def final_kernel(back_ref, one_ref, gate_ref, weight_ref, out_ref):
    channels = weight_ref.shape[0]
    combined = back_ref[...].reshape(channels, back_ref.shape[-1]).astype(F32)
    normed = normalized(combined, 0).astype(BF16)
    update = t_dot(normed, weight_ref[...])
    out_ref[...] = (one_ref[...] + gate_ref[...] * update).astype(BF16).reshape(out_ref.shape)


def exchanged(x):
    return lax.all_to_all(x, "res", split_axis=0, concat_axis=0, tiled=True)


def shards(
    homolog_symbol_ids,
    residue_attend_mask,
    alignment_state,
    pair,
    symbol_lookup_matrix,
    pair_bias_weight,
    row_projection_weight,
    horizontal_readout_matrix,
    column_projection_weight,
    vertical_readout_matrix,
    product_factor_matrices,
    outer_output_weight,
    triangle_input_weight,
    triangle_output_weight,
):
    devices = lax.axis_size("res")
    own_sequences, length, channels = alignment_state.shape
    sequences = own_sequences * devices
    own_rows, columns, pair_channels = pair.shape
    heads = pair_bias_weight.shape[1]
    width = product_factor_matrices.shape[1] // 2
    own_channels = pair_channels // devices
    rows = own_sequences * length

    groups = [list(range(first, devices, 2)) for first in range(2)]
    half = devices // 2
    second = (lax.axis_index("res") % 2).reshape(1)

    def among_class(x):
        return lax.all_to_all(x, "res", 0, 0, axis_index_groups=groups, tiled=True)

    def from_other_core(x):
        return lax.ppermute(x, "res", [(i, i ^ 1) for i in range(devices)])

    (bias,) = kernel_call(
        bias_kernel,
        [((half, own_rows * heads, columns), BF16)],
        (pair, pair_bias_weight.T),
        "bias",
        fetched=(0, 1),
    )
    bias = among_class(bias)
    factors = product_factor_matrices.T
    scores, value, gate, start, readout, wide = kernel_call(
        functools.partial(row_scores_kernel, heads=heads, own_rows=own_rows),
        [
            ((2 * own_sequences, length // 2 * heads, length), F32),
            ((2 * rows, channels), BF16),
            ((rows * max(1, 8 // own_rows), channels), F32),
            ((rows, channels), F32),
            ((channels, channels), BF16),
            ((width * own_rows, own_rows * channels), BF16),
        ],
        (
            second,
            homolog_symbol_ids,
            from_other_core(homolog_symbol_ids),
            residue_attend_mask.reshape(1, length),
            alignment_state,
            from_other_core(alignment_state),
            symbol_lookup_matrix,
            row_projection_weight,
            horizontal_readout_matrix,
            factors,
        ),
        "row_scores",
        flops=2 * rows * channels * 4 * channels,
        nbytes=1 << 21,
        scalars=1,
        fetched=(1, 3, 4, 6, 7, 8, 9),
    )
    (after_rows,) = kernel_call(
        functools.partial(row_mix_kernel, heads=heads, own_rows=own_rows),
        [((half, 2 * own_sequences * own_rows, channels), BF16)],
        (scores, bias, value, gate, start, readout),
        "row_mix",
    )
    by_residue = among_class(after_rows)
    per = max(1, 8 // own_rows)
    aligned, left, right = kernel_call(
        functools.partial(column_kernel, heads=heads, own_rows=own_rows),
        [
            ((sequences, own_rows, channels), BF16),
            ((sequences * own_rows, width), BF16),
            ((half, per * own_rows, width * sequences // per), BF16),
        ],
        (by_residue, column_projection_weight, vertical_readout_matrix, factors, wide),
        "column",
    )
    right = among_class(right)
    other = from_other_core(right)
    inside = pl.BlockSpec(memory_space=pltpu.VMEM)
    outside = pl.BlockSpec(memory_space=pl.ANY)
    spread, update, alignment_output = pl.pallas_call(
        functools.partial(spread_kernel, own_rows=own_rows, per=per),
        out_shape=(
            jax.ShapeDtypeStruct(
                (width * sequences // per, per * own_rows * pair_channels), BF16
            ),
            jax.ShapeDtypeStruct((half, own_rows, own_rows * pair_channels), F32),
            jax.ShapeDtypeStruct(aligned.shape, BF16),
        ),
        in_specs=[inside] * 4,
        out_specs=(inside, inside, outside),
        scratch_shapes=[pltpu.SemaphoreType.DMA],
        compiler_params=pltpu.CompilerParams(vmem_limit_bytes=VMEM_BYTES),
        cost_estimate=pl.CostEstimate(
            flops=2 * own_rows * sequences * width * width * pair_channels,
            bytes_accessed=1 << 21,
            transcendentals=0,
        ),
        name="spread",
    )(aligned, right, left, outer_output_weight.reshape(width, width * pair_channels))
    pair_one, gate_out, both = kernel_call(
        functools.partial(pair_kernel, sequences=sequences),
        [
            ((own_rows * columns, pair_channels), F32),
            ((own_rows * columns, pair_channels), F32),
            ((devices, own_channels, 2 * own_rows * columns), BF16),
        ],
        (
            second,
            update,
            other,
            spread,
            pair,
            triangle_input_weight[:, : 4 * pair_channels].T,
            triangle_input_weight[:, 4 * pair_channels :],
        ),
        "pair",
        scalars=1,
    )
    both = exchanged(both)
    (combined,) = kernel_call(
        functools.partial(triangle_kernel, own_rows=own_rows),
        [((devices, own_channels, own_rows * columns), BF16)],
        (both,),
        "triangle",
        scratch=[
            pltpu.VMEM((-(-columns // 128), pair_channels * own_rows, min(columns, 128)), F32)
        ]
        * 3,
    )
    back = exchanged(combined)
    (pair_output,) = kernel_call(
        final_kernel,
        [((own_rows, columns, pair_channels), BF16)],
        (back, pair_one, gate_out, triangle_output_weight),
        "final",
    )
    return (alignment_output, pair_output)


def solution(mesh):
    placed = (
        P(("crop", "res"), None),
        P("crop"),
        P(("crop", "res"), None, None),
        P(("crop", "res"), None, None),
    ) + (P(),) * 10
    return jax.shard_map(
        shards,
        mesh=mesh,
        in_specs=placed,
        out_specs=(P("crop", "res", None), P(("crop", "res"), None, None)),
        check_vma=False,
    )
```

```python
import functools

import jax
import jax.numpy as jnp
from jax import lax
from jax.experimental import pallas as pl
from jax.experimental.pallas import tpu as pltpu
from jax.sharding import PartitionSpec as P

EPSILON = 1e-05
F32 = jnp.float32
BF16 = jnp.bfloat16
VMEM_BYTES = 48 * 1024 * 1024


def normalized(rows, axis):
    average = jnp.mean(rows, axis, keepdims=True)
    centred = rows - average
    spread = jnp.mean(centred * centred, axis, keepdims=True)
    return centred * lax.rsqrt(spread + EPSILON)


def dot(a, b):
    return jnp.dot(a, b, preferred_element_type=F32)


def dot_t(a, b):
    return lax.dot_general(a, b, (((1,), (1,)), ((), ())), preferred_element_type=F32)


def t_dot(a, b):
    return lax.dot_general(a, b, (((0,), (0,)), ((), ())), preferred_element_type=F32)


def iota(shape, axis):
    return lax.broadcasted_iota(jnp.int32, shape, axis)


def selector(size, source_of):
    shape = (size, size)
    return (iota(shape, 1) == source_of(iota((size, 1), 0))).astype(F32).astype(BF16)


def swapped(outer, inner):
    return lambda p: (p % outer) * inner + p // outer


def lane_parts(channels, heads):
    lanes = min(128, channels)
    return [slice(at, at + lanes) for at in range(0, channels, lanes)], lanes * heads // channels


def own_channels_of(rows, lanes, width, first, own_rows):
    shape = (rows, lanes)
    return iota(shape, 0) // own_rows + first == iota(shape, 1) // width


def picked(pieces, masks):
    total = jnp.zeros_like(pieces[0])
    for piece, mask in zip(pieces, masks):
        total = jnp.where(jnp.broadcast_to(mask, piece.shape), piece, total)
    return total


def kernel_call(body, outs, args, name, flops=0, nbytes=0, scalars=0, fetched=(), late=(), scratch=()):
    inside = pl.BlockSpec(memory_space=pltpu.VMEM)
    outside = pl.BlockSpec(memory_space=pl.ANY)
    scalar = pl.BlockSpec(memory_space=pltpu.SMEM)
    args = [
        pltpu.with_memory_space_constraint(a, pltpu.HBM) if i in fetched else a
        for i, a in enumerate(args)
    ]

    def fetching(*refs):
        refs, held, sems = list(refs[: len(args) + len(outs)]), refs[len(args) + len(outs) : -1], refs[-1]
        copies = []
        for k, i in enumerate(fetched):
            copies.append(pltpu.make_async_copy(refs[i], held[k], sems.at[k]))
            copies[-1].start()
            refs[i] = held[k]
        later = [copy for copy, i in zip(copies, fetched) if i in late]
        for copy, i in zip(copies, fetched):
            if i not in late:
                copy.wait()
        if not late:
            return body(*refs)

        def arrive():
            for copy in later:
                copy.wait()

        return body(*refs, arrive=arrive)

    held = [pltpu.VMEM(args[i].shape, args[i].dtype) for i in fetched]
    if fetched:
        held.append(pltpu.SemaphoreType.DMA((len(fetched),)))
    return pl.pallas_call(
        fetching if fetched else body,
        out_shape=tuple(jax.ShapeDtypeStruct(s, d) for s, d in outs),
        in_specs=[
            scalar if i < scalars else outside if i in fetched else inside
            for i in range(len(args))
        ],
        out_specs=(inside,) * len(outs),
        scratch_shapes=held + list(scratch),
        compiler_params=pltpu.CompilerParams(vmem_limit_bytes=VMEM_BYTES),
        cost_estimate=pl.CostEstimate(flops=flops, bytes_accessed=nbytes, transcendentals=0),
        name=name,
    )(*args)


def bias_kernel(pair_ref, weight_ref, out_ref):
    rows, columns, channels = pair_ref.shape
    x = pair_ref[...].reshape(rows * columns, channels).astype(F32)
    normed = normalized(x, -1).astype(BF16)
    weight = weight_ref[...].astype(F32)
    heads = weight.shape[0]
    weight = jnp.broadcast_to(weight[:, None, :], (heads, rows, channels))
    weight = weight.reshape(heads * rows, channels).astype(BF16)
    bias = dot_t(weight, normed)
    row = iota((heads * rows, columns), 0) % rows
    block = bias[:, :columns]
    for i in range(1, rows):
        block = jnp.where(row == i, bias[:, i * columns : (i + 1) * columns], block)
    block = block.astype(BF16)
    for d in range(out_ref.shape[0]):
        out_ref[d] = block


def ordered(second, mine, other):
    flip = jnp.full(mine.shape, second, jnp.int32) == 1
    return jnp.where(flip, other, mine), jnp.where(flip, mine, other)


def row_scores_kernel(
    second_ref, ids_ref, other_ids_ref, mask_ref, state_ref, other_ref, table_ref, weight_ref,
    readout_ref, factor_ref,
    scores_ref, value_ref, gate_ref, start_ref, held_ref, wide_ref,
    *, heads, own_rows, arrive,
):
    own_sequences, length, channels = state_ref.shape
    tokens = table_ref.shape[0]
    second = second_ref[0]
    ids = jnp.concatenate(ordered(second, ids_ref[...], other_ids_ref[...]), 0)
    states = jnp.concatenate(
        ordered(second, state_ref[...].astype(F32), other_ref[...].astype(F32)), 0
    )
    sequences = 2 * own_sequences
    starts = []
    for s in range(sequences):
        hot = (iota((tokens, length), 0) == ids[s : s + 1, :]).astype(F32).astype(BF16)
        starts.append(states[s] + t_dot(hot, table_ref[...]))
    start = jnp.concatenate(starts, 0)
    normed = normalized(start, -1)
    arrive()
    held_ref[...] = readout_ref[...]
    projected = dot(normed.astype(BF16), weight_ref[:, channels : 3 * channels])
    key = projected[:, :channels].astype(BF16)
    value_ref[...] = projected[:, channels:].astype(BF16)

    def mine(x):
        pairs = x.reshape(sequences * length // (2 * own_rows), 2 * own_rows, channels)
        low, high = pairs[:, :own_rows], pairs[:, own_rows:]
        return ordered(second, low, high)[0].reshape(sequences * length // 2, channels)

    start_ref[...] = mine(start)
    own = mine(normed)
    per = max(1, 8 // own_rows)
    own = own.reshape(own.shape[0] // own_rows, own_rows, channels)
    own = jnp.concatenate([own] * per, 1).reshape(-1, channels).astype(BF16)
    query = dot(own, weight_ref[:, :channels]) * (channels // heads) ** (-0.5)
    query = query.astype(BF16).astype(F32)
    gate_ref[...] = jax.nn.sigmoid(dot(own, weight_ref[:, 3 * channels :]))
    extra = (mask_ref[...].astype(F32) - 1.0) * 10000.0
    tall = query.shape[0] // sequences
    block = per * own_rows
    parts, inner = lane_parts(channels, heads)
    masks = [
        own_channels_of(block, channels // len(parts), channels // heads, h, own_rows)[None]
        for h in range(0, inner, per)
    ]
    size = len(masks) * tall
    for s in range(sequences):
        for u, part in enumerate(parts):
            rows = query[s * tall : (s + 1) * tall, part]
            rows = rows.reshape(tall // block, block, rows.shape[1])
            spread = [
                picked([rows], [mask]).reshape(tall, rows.shape[2]).astype(BF16) for mask in masks
            ]
            scores_ref[s, u * size : (u + 1) * size] = (
                dot_t(jnp.concatenate(spread, 0), key[s * length : (s + 1) * length, part]) + extra
            )
    width = factor_ref.shape[0] // 2
    right = factor_ref[width:].astype(F32)
    repeated = jnp.broadcast_to(right[:, None, :], (width, own_rows, channels)).reshape(
        width * own_rows, channels
    )
    row = iota(repeated.shape, 0) % own_rows
    for r in range(own_rows):
        wide_ref[:, r * channels : (r + 1) * channels] = jnp.where(row == r, repeated, 0.0).astype(
            BF16
        )


def softmax_parts(scores):
    e = jnp.exp(scores - jnp.max(scores, -1, keepdims=True))
    return e.astype(BF16), 1.0 / jnp.sum(e, -1, keepdims=True)


def row_mix_kernel(
    scores_ref, bias_ref, value_ref, gate_ref, start_ref, weight_ref, out_ref, *, heads, own_rows
):
    sequences, expanded, length = scores_ref.shape
    channels = value_ref.shape[1]
    groups = out_ref.shape[0]
    per = max(1, 8 // own_rows)
    tiles = heads // per
    block = per * own_rows
    tall = groups * block
    bias = bias_ref[...].astype(F32)
    bias = jnp.concatenate(
        [
            bias[:, t * block : (t + 1) * block].reshape(tall, length)
            for t in range(tiles)
        ],
        0,
    )
    parts, inner = lane_parts(channels, heads)
    masks = [
        own_channels_of(block, channels // len(parts), channels // heads, h, own_rows)[None]
        for h in range(0, inner, per)
    ]
    size = len(masks) * tall
    pieces = []
    for s in range(sequences):
        weights, scale = softmax_parts(scores_ref[s] + bias)
        mixed = []
        for u, part in enumerate(parts):
            rows = slice(u * size, (u + 1) * size)
            whole = dot(weights[rows], value_ref[s * length : (s + 1) * length, part])
            whole = whole * scale[rows]
            whole = whole.reshape(len(masks), groups, block, whole.shape[1])
            mixed.append(
                picked([whole[t] for t in range(len(masks))], masks).reshape(tall, whole.shape[3])
            )
        mixed = jnp.concatenate(mixed, 1)
        gated = (gate_ref[s * tall : (s + 1) * tall] * mixed).astype(BF16)
        update = dot(gated, weight_ref[...]).reshape(groups, block, channels)
        after = start_ref[s * groups * own_rows : (s + 1) * groups * own_rows].reshape(
            groups, own_rows, channels
        )
        for h in range(per):
            after = after + update[:, h * own_rows : (h + 1) * own_rows]
        pieces.append(after)
    out_ref[...] = jnp.concatenate(pieces, 1).astype(BF16)


def column_kernel(
    state_ref, weight_ref, readout_ref, factor_ref, wide_ref, out_ref, left_ref, right_ref,
    *, heads, own_rows,
):
    devices, block, channels = state_ref.shape
    size = devices * block
    sequences = size // own_rows
    to_rows = selector(size, swapped(sequences, own_rows))
    to_sequences = selector(size, swapped(own_rows, sequences))
    start = dot(to_rows, state_ref[...].reshape(size, channels))
    centred = start - jnp.mean(start, -1, keepdims=True)
    inverse = lax.rsqrt(jnp.mean(centred * centred, -1, keepdims=True) + EPSILON)
    projected = dot(centred.astype(BF16), weight_ref[...]) * inverse
    query = (projected[:, :channels] * (channels // heads) ** (-0.5)).astype(BF16).astype(F32)
    key = projected[:, channels : 2 * channels].astype(BF16)
    value = projected[:, 2 * channels : 3 * channels].astype(BF16)
    gate = jax.nn.sigmoid(projected[:, 3 * channels :])
    parts, inner = lane_parts(channels, heads)
    masks = [
        own_channels_of(1, channels // len(parts), channels // heads, h, 1) for h in range(inner)
    ]
    gated = []
    for r in range(own_rows):
        rows = slice(r * sequences, (r + 1) * sequences)
        mixed = []
        for part in parts:
            spread = [picked([query[rows, part]], [mask]).astype(BF16) for mask in masks]
            weights, scale = softmax_parts(dot_t(jnp.concatenate(spread, 0), key[rows, part]))
            whole = dot(weights, value[rows, part]) * scale
            mixed.append(
                picked(
                    [whole[h * sequences : (h + 1) * sequences] for h in range(inner)], masks
                )
            )
        gated.append((gate[rows] * jnp.concatenate(mixed, 1)).astype(BF16))
    after = start + dot(jnp.concatenate(gated, 0), readout_ref[...])
    normed = normalized(after, -1).astype(BF16)
    width = factor_ref.shape[0] // 2
    fold = max(1, 128 // sequences)
    part = width // fold
    side = jnp.concatenate(
        [normed[r * sequences : (r + 1) * sequences] for r in range(own_rows)], 1
    )
    right = dot_t(wide_ref[...], side)
    cut = part * own_rows
    right = jnp.concatenate([right[f * cut : (f + 1) * cut] for f in range(fold)], 1)
    tall = right_ref.shape[1]
    packed = jnp.concatenate(
        [right[t * tall : (t + 1) * tall] for t in range(cut // tall)], 1
    ).astype(BF16)
    for d in range(right_ref.shape[0]):
        right_ref[d] = packed
    left_ref[...] = dot_t(normed, factor_ref[:width]).astype(BF16)
    out_ref[...] = dot(to_sequences, after.astype(BF16)).astype(BF16).reshape(out_ref.shape)


def half_update(right, spread, own_rows):
    groups, tall, lanes = right.shape
    columns = spread.shape[1] * own_rows // tall
    whole = dot(right.reshape(groups * tall, lanes), spread).reshape(groups, tall, -1)
    total = whole[:, :own_rows, :columns]
    for e in range(1, tall // own_rows):
        total = total + whole[
            :, e * own_rows : (e + 1) * own_rows, e * columns : (e + 1) * columns
        ]
    return total


def spread_kernel(
    aligned_ref, right_ref, left_ref, weight_ref, out_ref, half_ref, final_ref, sem,
    *, own_rows, per,
):
    store = pltpu.make_async_copy(aligned_ref, final_ref, sem)
    store.start()
    size, width = left_ref.shape
    sequences = size // own_rows
    channels = weight_ref.shape[1] // width
    fold = max(1, 128 // sequences)
    part = width // fold
    product = dot(left_ref[...], weight_ref[...])
    for d in range(width):
        f, t, e = d // part, d % part // per, d % per
        at = (t * fold + f) * sequences
        for r in range(own_rows):
            to = (e * own_rows + r) * channels
            out_ref[at : at + sequences, to : to + channels] = product[
                r * sequences : (r + 1) * sequences, d * channels : (d + 1) * channels
            ].astype(BF16)
    half_ref[...] = half_update(right_ref[...], out_ref[...], own_rows)
    store.wait()


def pair_kernel(
    second_ref, half_ref, other_ref, spread_ref, pair_ref, weight_ref, gate_weight_ref,
    one_ref, gate_ref, out_ref,
    *, sequences,
):
    own_rows, columns, channels = pair_ref.shape
    halves = ordered(
        second_ref[0], half_ref[...], half_update(other_ref[...], spread_ref[...], own_rows)
    )
    update = jnp.concatenate(halves, 1).reshape(columns, own_rows * channels) * (1.0 / sequences)
    ones = [
        pair_ref[i].astype(F32) + update[:, i * channels : (i + 1) * channels]
        for i in range(own_rows)
    ]
    one = jnp.concatenate(ones, 0)
    one_ref[...] = one
    normed = normalized(one, -1).astype(BF16)
    gate_ref[...] = jax.nn.sigmoid(dot(normed, gate_weight_ref[...]))
    factors = dot_t(weight_ref[...], normed)
    left = jax.nn.sigmoid(factors[channels : 2 * channels]) * factors[:channels]
    right = jax.nn.sigmoid(factors[3 * channels :]) * factors[2 * channels : 3 * channels]
    both = jnp.concatenate([left.astype(BF16), right.astype(BF16)], 1)
    out_ref[...] = both.reshape(out_ref.shape)


def triangle_kernel(both_ref, out_ref, left_ref, right_ref, ordered_ref, *, own_rows):
    devices, own_channels, lanes = both_ref.shape
    columns = lanes // 2 // own_rows
    size = devices * own_channels
    tile = left_ref.shape[2]
    tiles = columns // tile
    both = both_ref[...].reshape(size, lanes).astype(F32)
    for i in range(own_rows):
        rows = slice(i * size, (i + 1) * size)
        for k in range(tiles):
            at = i * columns + k * tile
            left_ref[k, rows] = both[:, at : at + tile]
            at += own_rows * columns
            right_ref[k, rows] = both[:, at : at + tile]

    def channel_rows(c, i):
        return pl.ds(i * size + c, devices, stride=own_channels)

    for k in range(tiles):
        for c in range(own_channels):
            for i in range(own_rows):
                ordered_ref[k, pl.ds(c * columns + i, devices, stride=own_rows), :] = right_ref[
                    k, channel_rows(c, i), :
                ]
    for c in range(own_channels):
        combined = jnp.zeros((columns, columns), F32)
        for k in range(tiles):
            left = jnp.concatenate(
                [left_ref[k, channel_rows(c, i), :] for i in range(own_rows)], 0
            )
            right = ordered_ref[k, c * columns : (c + 1) * columns]
            combined = combined + dot_t(left.astype(BF16), right.astype(BF16))
        for i in range(own_rows):
            for k in range(tiles):
                right_ref[k, channel_rows(c, i), :] = combined[
                    i * devices : (i + 1) * devices, k * tile : (k + 1) * tile
                ]
    out_ref[...] = (
        jnp.concatenate(
            [
                right_ref[k, i * size : (i + 1) * size]
                for i in range(own_rows)
                for k in range(tiles)
            ],
            1,
        )
        .astype(BF16)
        .reshape(out_ref.shape)
    )


def final_kernel(back_ref, one_ref, gate_ref, weight_ref, out_ref):
    channels = weight_ref.shape[0]
    combined = back_ref[...].reshape(channels, back_ref.shape[-1]).astype(F32)
    normed = normalized(combined, 0).astype(BF16)
    update = t_dot(normed, weight_ref[...])
    out_ref[...] = (one_ref[...] + gate_ref[...] * update).astype(BF16).reshape(out_ref.shape)


def exchanged(x):
    return lax.all_to_all(x, "res", split_axis=0, concat_axis=0, tiled=True)


def shards(
    homolog_symbol_ids,
    residue_attend_mask,
    alignment_state,
    pair,
    symbol_lookup_matrix,
    pair_bias_weight,
    row_projection_weight,
    horizontal_readout_matrix,
    column_projection_weight,
    vertical_readout_matrix,
    product_factor_matrices,
    outer_output_weight,
    triangle_input_weight,
    triangle_output_weight,
):
    devices = lax.axis_size("res")
    own_sequences, length, channels = alignment_state.shape
    sequences = own_sequences * devices
    own_rows, columns, pair_channels = pair.shape
    heads = pair_bias_weight.shape[1]
    width = product_factor_matrices.shape[1] // 2
    own_channels = pair_channels // devices
    rows = own_sequences * length

    groups = [list(range(first, devices, 2)) for first in range(2)]
    half = devices // 2
    second = (lax.axis_index("res") % 2).reshape(1)

    def among_class(x):
        return lax.all_to_all(x, "res", 0, 0, axis_index_groups=groups, tiled=True)

    def from_other_core(x):
        return lax.ppermute(x, "res", [(i, i ^ 1) for i in range(devices)])

    (bias,) = kernel_call(
        bias_kernel,
        [((half, own_rows * heads, columns), BF16)],
        (pair, pair_bias_weight.T),
        "bias",
        fetched=(0, 1),
    )
    bias = among_class(bias)
    factors = product_factor_matrices.T
    scores, value, gate, start, readout, wide = kernel_call(
        functools.partial(row_scores_kernel, heads=heads, own_rows=own_rows),
        [
            ((2 * own_sequences, length // 2 * heads, length), F32),
            ((2 * rows, channels), BF16),
            ((rows * max(1, 8 // own_rows), channels), F32),
            ((rows, channels), F32),
            ((channels, channels), BF16),
            ((width * own_rows, own_rows * channels), BF16),
        ],
        (
            second,
            homolog_symbol_ids,
            from_other_core(homolog_symbol_ids),
            residue_attend_mask.reshape(1, length),
            alignment_state,
            from_other_core(alignment_state),
            symbol_lookup_matrix,
            row_projection_weight,
            horizontal_readout_matrix,
            factors,
        ),
        "row_scores",
        flops=2 * rows * channels * 4 * channels,
        nbytes=1 << 21,
        scalars=1,
        fetched=(1, 3, 4, 6, 7, 8, 9),
        late=(3, 7, 8, 9),
    )
    (after_rows,) = kernel_call(
        functools.partial(row_mix_kernel, heads=heads, own_rows=own_rows),
        [((half, 2 * own_sequences * own_rows, channels), BF16)],
        (scores, bias, value, gate, start, readout),
        "row_mix",
    )
    by_residue = among_class(after_rows)
    per = max(1, 8 // own_rows)
    aligned, left, right = kernel_call(
        functools.partial(column_kernel, heads=heads, own_rows=own_rows),
        [
            ((sequences, own_rows, channels), BF16),
            ((sequences * own_rows, width), BF16),
            ((half, per * own_rows, width * sequences // per), BF16),
        ],
        (by_residue, column_projection_weight, vertical_readout_matrix, factors, wide),
        "column",
    )
    right = among_class(right)
    other = from_other_core(right)
    inside = pl.BlockSpec(memory_space=pltpu.VMEM)
    outside = pl.BlockSpec(memory_space=pl.ANY)
    spread, update, alignment_output = pl.pallas_call(
        functools.partial(spread_kernel, own_rows=own_rows, per=per),
        out_shape=(
            jax.ShapeDtypeStruct(
                (width * sequences // per, per * own_rows * pair_channels), BF16
            ),
            jax.ShapeDtypeStruct((half, own_rows, own_rows * pair_channels), F32),
            jax.ShapeDtypeStruct(aligned.shape, BF16),
        ),
        in_specs=[inside] * 4,
        out_specs=(inside, inside, outside),
        scratch_shapes=[pltpu.SemaphoreType.DMA],
        compiler_params=pltpu.CompilerParams(vmem_limit_bytes=VMEM_BYTES),
        cost_estimate=pl.CostEstimate(
            flops=2 * own_rows * sequences * width * width * pair_channels,
            bytes_accessed=1 << 21,
            transcendentals=0,
        ),
        name="spread",
    )(aligned, right, left, outer_output_weight.reshape(width, width * pair_channels))
    pair_one, gate_out, both = kernel_call(
        functools.partial(pair_kernel, sequences=sequences),
        [
            ((own_rows * columns, pair_channels), F32),
            ((own_rows * columns, pair_channels), F32),
            ((devices, own_channels, 2 * own_rows * columns), BF16),
        ],
        (
            second,
            update,
            other,
            spread,
            pair,
            triangle_input_weight[:, : 4 * pair_channels].T,
            triangle_input_weight[:, 4 * pair_channels :],
        ),
        "pair",
        scalars=1,
    )
    both = exchanged(both)
    (combined,) = kernel_call(
        functools.partial(triangle_kernel, own_rows=own_rows),
        [((devices, own_channels, own_rows * columns), BF16)],
        (both,),
        "triangle",
        scratch=[
            pltpu.VMEM((-(-columns // 128), pair_channels * own_rows, min(columns, 128)), F32)
        ]
        * 3,
    )
    back = exchanged(combined)
    (pair_output,) = kernel_call(
        final_kernel,
        [((own_rows, columns, pair_channels), BF16)],
        (back, pair_one, gate_out, triangle_output_weight),
        "final",
    )
    return (alignment_output, pair_output)


def solution(mesh):
    placed = (
        P(("crop", "res"), None),
        P("crop"),
        P(("crop", "res"), None, None),
        P(("crop", "res"), None, None),
    ) + (P(),) * 10
    return jax.shard_map(
        shards,
        mesh=mesh,
        in_specs=placed,
        out_specs=(P("crop", "res", None), P(("crop", "res"), None, None)),
        check_vma=False,
    )
```

```python
import functools

import jax
import jax.numpy as jnp
from jax import lax
from jax.experimental import pallas as pl
from jax.experimental.pallas import tpu as pltpu
from jax.sharding import PartitionSpec as P

EPSILON = 1e-05
F32 = jnp.float32
BF16 = jnp.bfloat16
VMEM_BYTES = 48 * 1024 * 1024


def normalized(rows, axis):
    average = jnp.mean(rows, axis, keepdims=True)
    centred = rows - average
    spread = jnp.mean(centred * centred, axis, keepdims=True)
    return centred * lax.rsqrt(spread + EPSILON)


def dot(a, b):
    return jnp.dot(a, b, preferred_element_type=F32)


def dot_t(a, b):
    return lax.dot_general(a, b, (((1,), (1,)), ((), ())), preferred_element_type=F32)


def t_dot(a, b):
    return lax.dot_general(a, b, (((0,), (0,)), ((), ())), preferred_element_type=F32)


def iota(shape, axis):
    return lax.broadcasted_iota(jnp.int32, shape, axis)


def selector(size, source_of):
    shape = (size, size)
    return (iota(shape, 1) == source_of(iota((size, 1), 0))).astype(F32).astype(BF16)


def swapped(outer, inner):
    return lambda p: (p % outer) * inner + p // outer


def lane_parts(channels, heads):
    lanes = min(128, channels)
    return [slice(at, at + lanes) for at in range(0, channels, lanes)], lanes * heads // channels


def own_channels_of(rows, lanes, width, first, own_rows):
    shape = (rows, lanes)
    return iota(shape, 0) // own_rows + first == iota(shape, 1) // width


def picked(pieces, masks):
    total = jnp.zeros_like(pieces[0])
    for piece, mask in zip(pieces, masks):
        total = jnp.where(jnp.broadcast_to(mask, piece.shape), piece, total)
    return total


def kernel_call(body, outs, args, name, flops=0, nbytes=0, scalars=0, fetched=(), late=(), scratch=()):
    inside = pl.BlockSpec(memory_space=pltpu.VMEM)
    outside = pl.BlockSpec(memory_space=pl.ANY)
    scalar = pl.BlockSpec(memory_space=pltpu.SMEM)
    args = [
        pltpu.with_memory_space_constraint(a, pltpu.HBM) if i in fetched else a
        for i, a in enumerate(args)
    ]

    def fetching(*refs):
        refs, held, sems = list(refs[: len(args) + len(outs)]), refs[len(args) + len(outs) : -1], refs[-1]
        copies = []
        for k, i in enumerate(fetched):
            copies.append(pltpu.make_async_copy(refs[i], held[k], sems.at[k]))
            copies[-1].start()
            refs[i] = held[k]
        later = [copy for copy, i in zip(copies, fetched) if i in late]
        for copy, i in zip(copies, fetched):
            if i not in late:
                copy.wait()
        if not late:
            return body(*refs)

        def arrive():
            for copy in later:
                copy.wait()

        return body(*refs, arrive=arrive)

    held = [pltpu.VMEM(args[i].shape, args[i].dtype) for i in fetched]
    if fetched:
        held.append(pltpu.SemaphoreType.DMA((len(fetched),)))
    return pl.pallas_call(
        fetching if fetched else body,
        out_shape=tuple(jax.ShapeDtypeStruct(s, d) for s, d in outs),
        in_specs=[
            scalar if i < scalars else outside if i in fetched else inside
            for i in range(len(args))
        ],
        out_specs=(inside,) * len(outs),
        scratch_shapes=held + list(scratch),
        compiler_params=pltpu.CompilerParams(vmem_limit_bytes=VMEM_BYTES),
        cost_estimate=pl.CostEstimate(flops=flops, bytes_accessed=nbytes, transcendentals=0),
        name=name,
    )(*args)


def bias_kernel(pair_ref, weight_ref, out_ref):
    rows, columns, channels = pair_ref.shape
    x = pair_ref[...].reshape(rows * columns, channels).astype(F32)
    normed = normalized(x, -1).astype(BF16)
    weight = weight_ref[...].astype(F32)
    heads = weight.shape[0]
    weight = jnp.broadcast_to(weight[:, None, :], (heads, rows, channels))
    weight = weight.reshape(heads * rows, channels).astype(BF16)
    bias = dot_t(weight, normed)
    row = iota((heads * rows, columns), 0) % rows
    block = bias[:, :columns]
    for i in range(1, rows):
        block = jnp.where(row == i, bias[:, i * columns : (i + 1) * columns], block)
    block = block.astype(BF16)
    for d in range(out_ref.shape[0]):
        out_ref[d] = block


def ordered(second, mine, other):
    flip = jnp.full(mine.shape, second, jnp.int32) == 1
    return jnp.where(flip, other, mine), jnp.where(flip, mine, other)


def own_scores_kernel(
    second_ref, ids_ref, mask_ref, state_ref, table_ref, weight_ref, readout_ref, factor_ref,
    scores_ref, value_ref, gate_ref, start_ref,
    held_mask_ref, held_table_ref, held_weight_ref, held_ref, wide_ref,
    *, heads, own_rows, arrive,
):
    row_scores(
        second_ref, ids_ref, mask_ref, state_ref, table_ref, weight_ref,
        scores_ref, value_ref, gate_ref, start_ref,
        heads=heads, own_rows=own_rows, arrive=arrive,
    )
    held_mask_ref[...] = mask_ref[...]
    held_table_ref[...] = table_ref[...]
    held_weight_ref[...] = weight_ref[...]
    held_ref[...] = readout_ref[...]
    widen(factor_ref, wide_ref, own_rows)


def other_scores_kernel(
    second_ref, ids_ref, mask_ref, state_ref, table_ref, weight_ref,
    scores_ref, value_ref, gate_ref, start_ref,
    *, heads, own_rows,
):
    row_scores(
        second_ref, ids_ref, mask_ref, state_ref, table_ref, weight_ref,
        scores_ref, value_ref, gate_ref, start_ref,
        heads=heads, own_rows=own_rows, arrive=None,
    )


def row_scores(
    second_ref, ids_ref, mask_ref, state_ref, table_ref, weight_ref,
    scores_ref, value_ref, gate_ref, start_ref,
    *, heads, own_rows, arrive,
):
    sequences, length, channels = state_ref.shape
    tokens = table_ref.shape[0]
    second = second_ref[0]
    ids = ids_ref[...]
    states = state_ref[...].astype(F32)
    starts = []
    for s in range(sequences):
        hot = (iota((tokens, length), 0) == ids[s : s + 1, :]).astype(F32).astype(BF16)
        starts.append(states[s] + t_dot(hot, table_ref[...]))
    start = jnp.concatenate(starts, 0)
    normed = normalized(start, -1)
    if arrive is not None:
        arrive()
    projected = dot(normed.astype(BF16), weight_ref[:, channels : 3 * channels])
    key = projected[:, :channels].astype(BF16)
    value_ref[...] = projected[:, channels:].astype(BF16)

    def mine(x):
        pairs = x.reshape(sequences * length // (2 * own_rows), 2 * own_rows, channels)
        low, high = pairs[:, :own_rows], pairs[:, own_rows:]
        return ordered(second, low, high)[0].reshape(sequences * length // 2, channels)

    start_ref[...] = mine(start)
    own = mine(normed)
    per = max(1, 8 // own_rows)
    own = own.reshape(own.shape[0] // own_rows, own_rows, channels)
    own = jnp.concatenate([own] * per, 1).reshape(-1, channels).astype(BF16)
    query = dot(own, weight_ref[:, :channels]) * (channels // heads) ** (-0.5)
    query = query.astype(BF16).astype(F32)
    gate_ref[...] = jax.nn.sigmoid(dot(own, weight_ref[:, 3 * channels :]))
    extra = (mask_ref[...].astype(F32) - 1.0) * 10000.0
    tall = query.shape[0] // sequences
    block = per * own_rows
    parts, inner = lane_parts(channels, heads)
    masks = [
        own_channels_of(block, channels // len(parts), channels // heads, h, own_rows)[None]
        for h in range(0, inner, per)
    ]
    size = len(masks) * tall
    for s in range(sequences):
        for u, part in enumerate(parts):
            rows = query[s * tall : (s + 1) * tall, part]
            rows = rows.reshape(tall // block, block, rows.shape[1])
            spread = [
                picked([rows], [mask]).reshape(tall, rows.shape[2]).astype(BF16) for mask in masks
            ]
            scores_ref[s, u * size : (u + 1) * size] = (
                dot_t(jnp.concatenate(spread, 0), key[s * length : (s + 1) * length, part]) + extra
            )

def widen(factor_ref, wide_ref, own_rows):
    width, channels = factor_ref.shape[0] // 2, factor_ref.shape[1]
    right = factor_ref[width:].astype(F32)
    repeated = jnp.broadcast_to(right[:, None, :], (width, own_rows, channels)).reshape(
        width * own_rows, channels
    )
    row = iota(repeated.shape, 0) % own_rows
    for r in range(own_rows):
        wide_ref[:, r * channels : (r + 1) * channels] = jnp.where(row == r, repeated, 0.0).astype(
            BF16
        )


def softmax_parts(scores):
    e = jnp.exp(scores - jnp.max(scores, -1, keepdims=True))
    return e.astype(BF16), 1.0 / jnp.sum(e, -1, keepdims=True)


def row_mix_kernel(
    second_ref, own_scores_ref, own_value_ref, own_gate_ref, own_start_ref,
    other_scores_ref, other_value_ref, other_gate_ref, other_start_ref,
    bias_ref, weight_ref, out_ref,
    *, heads, own_rows,
):
    sequences, expanded, length = own_scores_ref.shape
    value_ref = own_value_ref
    channels = value_ref.shape[1]
    groups = out_ref.shape[0]
    per = max(1, 8 // own_rows)
    tiles = heads // per
    block = per * own_rows
    tall = groups * block
    bias = bias_ref[...].astype(F32)
    bias = jnp.concatenate(
        [
            bias[:, t * block : (t + 1) * block].reshape(tall, length)
            for t in range(tiles)
        ],
        0,
    )
    parts, inner = lane_parts(channels, heads)
    masks = [
        own_channels_of(block, channels // len(parts), channels // heads, h, own_rows)[None]
        for h in range(0, inner, per)
    ]
    size = len(masks) * tall
    pieces = []
    sets = (
        (own_scores_ref, own_value_ref, own_gate_ref, own_start_ref),
        (other_scores_ref, other_value_ref, other_gate_ref, other_start_ref),
    )
    for (scores_ref, value_ref, gate_ref, start_ref), s in [
        (refs, s) for refs in sets for s in range(sequences)
    ]:
        weights, scale = softmax_parts(scores_ref[s] + bias)
        mixed = []
        for u, part in enumerate(parts):
            rows = slice(u * size, (u + 1) * size)
            whole = dot(weights[rows], value_ref[s * length : (s + 1) * length, part])
            whole = whole * scale[rows]
            whole = whole.reshape(len(masks), groups, block, whole.shape[1])
            mixed.append(
                picked([whole[t] for t in range(len(masks))], masks).reshape(tall, whole.shape[3])
            )
        mixed = jnp.concatenate(mixed, 1)
        gated = (gate_ref[s * tall : (s + 1) * tall] * mixed).astype(BF16)
        update = dot(gated, weight_ref[...]).reshape(groups, block, channels)
        after = start_ref[s * groups * own_rows : (s + 1) * groups * own_rows].reshape(
            groups, own_rows, channels
        )
        for h in range(per):
            after = after + update[:, h * own_rows : (h + 1) * own_rows]
        pieces.append(after)
    own, other = jnp.concatenate(pieces[:sequences], 1), jnp.concatenate(pieces[sequences:], 1)
    out_ref[...] = jnp.concatenate(ordered(second_ref[0], own, other), 1).astype(BF16)


def column_kernel(
    state_ref, weight_ref, readout_ref, factor_ref, wide_ref, out_ref, left_ref, right_ref,
    *, heads, own_rows,
):
    devices, block, channels = state_ref.shape
    size = devices * block
    sequences = size // own_rows
    to_rows = selector(size, swapped(sequences, own_rows))
    to_sequences = selector(size, swapped(own_rows, sequences))
    start = dot(to_rows, state_ref[...].reshape(size, channels))
    centred = start - jnp.mean(start, -1, keepdims=True)
    inverse = lax.rsqrt(jnp.mean(centred * centred, -1, keepdims=True) + EPSILON)
    projected = dot(centred.astype(BF16), weight_ref[...]) * inverse
    query = (projected[:, :channels] * (channels // heads) ** (-0.5)).astype(BF16).astype(F32)
    key = projected[:, channels : 2 * channels].astype(BF16)
    value = projected[:, 2 * channels : 3 * channels].astype(BF16)
    gate = jax.nn.sigmoid(projected[:, 3 * channels :])
    parts, inner = lane_parts(channels, heads)
    masks = [
        own_channels_of(1, channels // len(parts), channels // heads, h, 1) for h in range(inner)
    ]
    gated = []
    for r in range(own_rows):
        rows = slice(r * sequences, (r + 1) * sequences)
        mixed = []
        for part in parts:
            spread = [picked([query[rows, part]], [mask]).astype(BF16) for mask in masks]
            weights, scale = softmax_parts(dot_t(jnp.concatenate(spread, 0), key[rows, part]))
            whole = dot(weights, value[rows, part]) * scale
            mixed.append(
                picked(
                    [whole[h * sequences : (h + 1) * sequences] for h in range(inner)], masks
                )
            )
        gated.append((gate[rows] * jnp.concatenate(mixed, 1)).astype(BF16))
    after = start + dot(jnp.concatenate(gated, 0), readout_ref[...])
    normed = normalized(after, -1).astype(BF16)
    width = factor_ref.shape[0] // 2
    fold = max(1, 128 // sequences)
    part = width // fold
    side = jnp.concatenate(
        [normed[r * sequences : (r + 1) * sequences] for r in range(own_rows)], 1
    )
    right = dot_t(wide_ref[...], side)
    cut = part * own_rows
    right = jnp.concatenate([right[f * cut : (f + 1) * cut] for f in range(fold)], 1)
    tall = right_ref.shape[1]
    packed = jnp.concatenate(
        [right[t * tall : (t + 1) * tall] for t in range(cut // tall)], 1
    ).astype(BF16)
    for d in range(right_ref.shape[0]):
        right_ref[d] = packed
    left_ref[...] = dot_t(normed, factor_ref[:width]).astype(BF16)
    out_ref[...] = dot(to_sequences, after.astype(BF16)).astype(BF16).reshape(out_ref.shape)


def half_update(right, spread, own_rows):
    groups, tall, lanes = right.shape
    columns = spread.shape[1] * own_rows // tall
    whole = dot(right.reshape(groups * tall, lanes), spread).reshape(groups, tall, -1)
    total = whole[:, :own_rows, :columns]
    for e in range(1, tall // own_rows):
        total = total + whole[
            :, e * own_rows : (e + 1) * own_rows, e * columns : (e + 1) * columns
        ]
    return total


def spread_kernel(
    aligned_ref, right_ref, left_ref, weight_ref, out_ref, half_ref, final_ref, sem,
    *, own_rows, per,
):
    store = pltpu.make_async_copy(aligned_ref, final_ref, sem)
    store.start()
    size, width = left_ref.shape
    sequences = size // own_rows
    channels = weight_ref.shape[1] // width
    fold = max(1, 128 // sequences)
    part = width // fold
    product = dot(left_ref[...], weight_ref[...])
    for d in range(width):
        f, t, e = d // part, d % part // per, d % per
        at = (t * fold + f) * sequences
        for r in range(own_rows):
            to = (e * own_rows + r) * channels
            out_ref[at : at + sequences, to : to + channels] = product[
                r * sequences : (r + 1) * sequences, d * channels : (d + 1) * channels
            ].astype(BF16)
    half_ref[...] = half_update(right_ref[...], out_ref[...], own_rows)
    store.wait()


def pair_kernel(
    second_ref, half_ref, other_ref, spread_ref, pair_ref, weight_ref, gate_weight_ref,
    one_ref, gate_ref, out_ref,
    *, sequences,
):
    own_rows, columns, channels = pair_ref.shape
    halves = ordered(
        second_ref[0], half_ref[...], half_update(other_ref[...], spread_ref[...], own_rows)
    )
    update = jnp.concatenate(halves, 1).reshape(columns, own_rows * channels) * (1.0 / sequences)
    ones = [
        pair_ref[i].astype(F32) + update[:, i * channels : (i + 1) * channels]
        for i in range(own_rows)
    ]
    one = jnp.concatenate(ones, 0)
    one_ref[...] = one
    normed = normalized(one, -1).astype(BF16)
    gate_ref[...] = jax.nn.sigmoid(dot(normed, gate_weight_ref[...]))
    factors = dot_t(weight_ref[...], normed)
    left = jax.nn.sigmoid(factors[channels : 2 * channels]) * factors[:channels]
    right = jax.nn.sigmoid(factors[3 * channels :]) * factors[2 * channels : 3 * channels]
    both = jnp.concatenate([left.astype(BF16), right.astype(BF16)], 1)
    out_ref[...] = both.reshape(out_ref.shape)


def triangle_kernel(both_ref, out_ref, left_ref, right_ref, ordered_ref, *, own_rows):
    devices, own_channels, lanes = both_ref.shape
    columns = lanes // 2 // own_rows
    size = devices * own_channels
    tile = left_ref.shape[2]
    tiles = columns // tile
    both = both_ref[...].reshape(size, lanes).astype(F32)
    for i in range(own_rows):
        rows = slice(i * size, (i + 1) * size)
        for k in range(tiles):
            at = i * columns + k * tile
            left_ref[k, rows] = both[:, at : at + tile]
            at += own_rows * columns
            right_ref[k, rows] = both[:, at : at + tile]

    def channel_rows(c, i):
        return pl.ds(i * size + c, devices, stride=own_channels)

    for k in range(tiles):
        for c in range(own_channels):
            for i in range(own_rows):
                ordered_ref[k, pl.ds(c * columns + i, devices, stride=own_rows), :] = right_ref[
                    k, channel_rows(c, i), :
                ]
    for c in range(own_channels):
        combined = jnp.zeros((columns, columns), F32)
        for k in range(tiles):
            left = jnp.concatenate(
                [left_ref[k, channel_rows(c, i), :] for i in range(own_rows)], 0
            )
            right = ordered_ref[k, c * columns : (c + 1) * columns]
            combined = combined + dot_t(left.astype(BF16), right.astype(BF16))
        for i in range(own_rows):
            for k in range(tiles):
                right_ref[k, channel_rows(c, i), :] = combined[
                    i * devices : (i + 1) * devices, k * tile : (k + 1) * tile
                ]
    out_ref[...] = (
        jnp.concatenate(
            [
                right_ref[k, i * size : (i + 1) * size]
                for i in range(own_rows)
                for k in range(tiles)
            ],
            1,
        )
        .astype(BF16)
        .reshape(out_ref.shape)
    )


def final_kernel(back_ref, one_ref, gate_ref, weight_ref, out_ref):
    channels = weight_ref.shape[0]
    combined = back_ref[...].reshape(channels, back_ref.shape[-1]).astype(F32)
    normed = normalized(combined, 0).astype(BF16)
    update = t_dot(normed, weight_ref[...])
    out_ref[...] = (one_ref[...] + gate_ref[...] * update).astype(BF16).reshape(out_ref.shape)


def exchanged(x):
    return lax.all_to_all(x, "res", split_axis=0, concat_axis=0, tiled=True)


def shards(
    homolog_symbol_ids,
    residue_attend_mask,
    alignment_state,
    pair,
    symbol_lookup_matrix,
    pair_bias_weight,
    row_projection_weight,
    horizontal_readout_matrix,
    column_projection_weight,
    vertical_readout_matrix,
    product_factor_matrices,
    outer_output_weight,
    triangle_input_weight,
    triangle_output_weight,
):
    devices = lax.axis_size("res")
    own_sequences, length, channels = alignment_state.shape
    sequences = own_sequences * devices
    own_rows, columns, pair_channels = pair.shape
    heads = pair_bias_weight.shape[1]
    width = product_factor_matrices.shape[1] // 2
    own_channels = pair_channels // devices
    rows = own_sequences * length

    groups = [list(range(first, devices, 2)) for first in range(2)]
    half = devices // 2
    second = (lax.axis_index("res") % 2).reshape(1)

    def among_class(x):
        return lax.all_to_all(x, "res", 0, 0, axis_index_groups=groups, tiled=True)

    def from_other_core(x):
        return lax.ppermute(x, "res", [(i, i ^ 1) for i in range(devices)])

    (bias,) = kernel_call(
        bias_kernel,
        [((half, own_rows * heads, columns), BF16)],
        (pair, pair_bias_weight.T),
        "bias",
        fetched=(0, 1),
    )
    bias = among_class(bias)
    factors = product_factor_matrices.T
    parts = [
        ((own_sequences, half * own_rows * heads, length), F32),
        ((rows, channels), BF16),
        ((rows // 2 * max(1, 8 // own_rows), channels), F32),
        ((rows // 2, channels), F32),
    ]
    estimate = dict(flops=2 * rows * channels * 4 * channels, nbytes=1 << 21)
    *own, mask, table, row_weight, readout, wide = kernel_call(
        functools.partial(own_scores_kernel, heads=heads, own_rows=own_rows),
        parts
        + [
            ((1, length), jnp.int32),
            (symbol_lookup_matrix.shape, BF16),
            (row_projection_weight.shape, BF16),
            ((channels, channels), BF16),
            ((width * own_rows, own_rows * channels), BF16),
        ],
        (
            second,
            homolog_symbol_ids,
            residue_attend_mask.reshape(1, length),
            alignment_state,
            symbol_lookup_matrix,
            row_projection_weight,
            horizontal_readout_matrix,
            factors,
        ),
        "own_scores",
        scalars=1,
        fetched=(1, 3, 4, 2, 5, 6, 7),
        late=(2, 5, 6, 7),
        **estimate,
    )
    other_scores = kernel_call(
        functools.partial(other_scores_kernel, heads=heads, own_rows=own_rows),
        parts,
        (
            second,
            from_other_core(homolog_symbol_ids),
            mask,
            from_other_core(alignment_state),
            table,
            row_weight,
        ),
        "other_scores",
        scalars=1,
        **estimate,
    )
    (after_rows,) = kernel_call(
        functools.partial(row_mix_kernel, heads=heads, own_rows=own_rows),
        [((half, 2 * own_sequences * own_rows, channels), BF16)],
        (second, *own, *other_scores, bias, readout),
        "row_mix",
        scalars=1,
    )
    by_residue = among_class(after_rows)
    per = max(1, 8 // own_rows)
    aligned, left, right = kernel_call(
        functools.partial(column_kernel, heads=heads, own_rows=own_rows),
        [
            ((sequences, own_rows, channels), BF16),
            ((sequences * own_rows, width), BF16),
            ((half, per * own_rows, width * sequences // per), BF16),
        ],
        (by_residue, column_projection_weight, vertical_readout_matrix, factors, wide),
        "column",
    )
    right = among_class(right)
    other = from_other_core(right)
    inside = pl.BlockSpec(memory_space=pltpu.VMEM)
    outside = pl.BlockSpec(memory_space=pl.ANY)
    spread, update, alignment_output = pl.pallas_call(
        functools.partial(spread_kernel, own_rows=own_rows, per=per),
        out_shape=(
            jax.ShapeDtypeStruct(
                (width * sequences // per, per * own_rows * pair_channels), BF16
            ),
            jax.ShapeDtypeStruct((half, own_rows, own_rows * pair_channels), F32),
            jax.ShapeDtypeStruct(aligned.shape, BF16),
        ),
        in_specs=[inside] * 4,
        out_specs=(inside, inside, outside),
        scratch_shapes=[pltpu.SemaphoreType.DMA],
        compiler_params=pltpu.CompilerParams(vmem_limit_bytes=VMEM_BYTES),
        cost_estimate=pl.CostEstimate(
            flops=2 * own_rows * sequences * width * width * pair_channels,
            bytes_accessed=1 << 21,
            transcendentals=0,
        ),
        name="spread",
    )(aligned, right, left, outer_output_weight.reshape(width, width * pair_channels))
    pair_one, gate_out, both = kernel_call(
        functools.partial(pair_kernel, sequences=sequences),
        [
            ((own_rows * columns, pair_channels), F32),
            ((own_rows * columns, pair_channels), F32),
            ((devices, own_channels, 2 * own_rows * columns), BF16),
        ],
        (
            second,
            update,
            other,
            spread,
            pair,
            triangle_input_weight[:, : 4 * pair_channels].T,
            triangle_input_weight[:, 4 * pair_channels :],
        ),
        "pair",
        scalars=1,
    )
    both = exchanged(both)
    (combined,) = kernel_call(
        functools.partial(triangle_kernel, own_rows=own_rows),
        [((devices, own_channels, own_rows * columns), BF16)],
        (both,),
        "triangle",
        scratch=[
            pltpu.VMEM((-(-columns // 128), pair_channels * own_rows, min(columns, 128)), F32)
        ]
        * 3,
    )
    back = exchanged(combined)
    (pair_output,) = kernel_call(
        final_kernel,
        [((own_rows, columns, pair_channels), BF16)],
        (back, pair_one, gate_out, triangle_output_weight),
        "final",
    )
    return (alignment_output, pair_output)


def solution(mesh):
    placed = (
        P(("crop", "res"), None),
        P("crop"),
        P(("crop", "res"), None, None),
        P(("crop", "res"), None, None),
    ) + (P(),) * 10
    return jax.shard_map(
        shards,
        mesh=mesh,
        in_specs=placed,
        out_specs=(P("crop", "res", None), P(("crop", "res"), None, None)),
        check_vma=False,
    )
```

```python
import functools

import jax
import jax.numpy as jnp
from jax import lax
from jax.experimental import pallas as pl
from jax.experimental.pallas import tpu as pltpu
from jax.sharding import PartitionSpec as P

EPSILON = 1e-05
F32 = jnp.float32
BF16 = jnp.bfloat16
VMEM_BYTES = 48 * 1024 * 1024


def normalized(rows, axis):
    average = jnp.mean(rows, axis, keepdims=True)
    centred = rows - average
    spread = jnp.mean(centred * centred, axis, keepdims=True)
    return centred * lax.rsqrt(spread + EPSILON)


def dot(a, b):
    return jnp.dot(a, b, preferred_element_type=F32)


def dot_t(a, b):
    return lax.dot_general(a, b, (((1,), (1,)), ((), ())), preferred_element_type=F32)


def t_dot(a, b):
    return lax.dot_general(a, b, (((0,), (0,)), ((), ())), preferred_element_type=F32)


def iota(shape, axis):
    return lax.broadcasted_iota(jnp.int32, shape, axis)


def selector(size, source_of):
    shape = (size, size)
    return (iota(shape, 1) == source_of(iota((size, 1), 0))).astype(F32).astype(BF16)


def swapped(outer, inner):
    return lambda p: (p % outer) * inner + p // outer


def lane_parts(channels, heads):
    lanes = min(128, channels)
    return [slice(at, at + lanes) for at in range(0, channels, lanes)], lanes * heads // channels


def own_channels_of(rows, lanes, width, first, own_rows):
    shape = (rows, lanes)
    return iota(shape, 0) // own_rows + first == iota(shape, 1) // width


def picked(pieces, masks):
    total = jnp.zeros_like(pieces[0])
    for piece, mask in zip(pieces, masks):
        total = jnp.where(jnp.broadcast_to(mask, piece.shape), piece, total)
    return total


def kernel_call(body, outs, args, name, flops=0, nbytes=0, scalars=0, fetched=(), late=(), scratch=()):
    inside = pl.BlockSpec(memory_space=pltpu.VMEM)
    outside = pl.BlockSpec(memory_space=pl.ANY)
    scalar = pl.BlockSpec(memory_space=pltpu.SMEM)
    args = [
        pltpu.with_memory_space_constraint(a, pltpu.HBM) if i in fetched else a
        for i, a in enumerate(args)
    ]

    def fetching(*refs):
        refs, held, sems = list(refs[: len(args) + len(outs)]), refs[len(args) + len(outs) : -1], refs[-1]
        copies = []
        for k, i in enumerate(fetched):
            copies.append(pltpu.make_async_copy(refs[i], held[k], sems.at[k]))
            copies[-1].start()
            refs[i] = held[k]
        later = [copy for copy, i in zip(copies, fetched) if i in late]
        for copy, i in zip(copies, fetched):
            if i not in late:
                copy.wait()
        if not late:
            return body(*refs)

        def arrive():
            for copy in later:
                copy.wait()

        return body(*refs, arrive=arrive)

    held = [pltpu.VMEM(args[i].shape, args[i].dtype) for i in fetched]
    if fetched:
        held.append(pltpu.SemaphoreType.DMA((len(fetched),)))
    return pl.pallas_call(
        fetching if fetched else body,
        out_shape=tuple(jax.ShapeDtypeStruct(s, d) for s, d in outs),
        in_specs=[
            scalar if i < scalars else outside if i in fetched else inside
            for i in range(len(args))
        ],
        out_specs=(inside,) * len(outs),
        scratch_shapes=held + list(scratch),
        compiler_params=pltpu.CompilerParams(vmem_limit_bytes=VMEM_BYTES),
        cost_estimate=pl.CostEstimate(flops=flops, bytes_accessed=nbytes, transcendentals=0),
        name=name,
    )(*args)


def bias_kernel(pair_ref, weight_ref, out_ref):
    rows, columns, channels = pair_ref.shape
    x = pair_ref[...].reshape(rows * columns, channels).astype(F32)
    normed = normalized(x, -1).astype(BF16)
    weight = weight_ref[...].astype(F32)
    heads = weight.shape[0]
    weight = jnp.broadcast_to(weight[:, None, :], (heads, rows, channels))
    weight = weight.reshape(heads * rows, channels).astype(BF16)
    bias = dot_t(weight, normed)
    row = iota((heads * rows, columns), 0) % rows
    block = bias[:, :columns]
    for i in range(1, rows):
        block = jnp.where(row == i, bias[:, i * columns : (i + 1) * columns], block)
    block = block.astype(BF16)
    for d in range(out_ref.shape[0]):
        out_ref[d] = block


def ordered(second, mine, other):
    flip = jnp.full(mine.shape, second, jnp.int32) == 1
    return jnp.where(flip, other, mine), jnp.where(flip, mine, other)


def own_scores_kernel(
    second_ref, ids_ref, mask_ref, state_ref, table_ref, weight_ref, readout_ref, factor_ref,
    scores_ref, value_ref, gate_ref, start_ref,
    held_mask_ref, held_table_ref, held_weight_ref, held_ref, wide_ref,
    *, heads, own_rows, arrive,
):
    row_scores(
        second_ref, ids_ref, mask_ref, state_ref, table_ref, weight_ref,
        scores_ref, value_ref, gate_ref, start_ref,
        heads=heads, own_rows=own_rows, arrive=arrive,
    )
    held_mask_ref[...] = mask_ref[...]
    held_table_ref[...] = table_ref[...]
    held_weight_ref[...] = weight_ref[...]
    held_ref[...] = readout_ref[...]
    widen(factor_ref, wide_ref, own_rows)


def other_scores_kernel(
    second_ref, ids_ref, mask_ref, state_ref, table_ref, weight_ref,
    scores_ref, value_ref, gate_ref, start_ref,
    *, heads, own_rows,
):
    row_scores(
        second_ref, ids_ref, mask_ref, state_ref, table_ref, weight_ref,
        scores_ref, value_ref, gate_ref, start_ref,
        heads=heads, own_rows=own_rows, arrive=None,
    )


def row_scores(
    second_ref, ids_ref, mask_ref, state_ref, table_ref, weight_ref,
    scores_ref, value_ref, gate_ref, start_ref,
    *, heads, own_rows, arrive,
):
    sequences, length, channels = state_ref.shape
    tokens = table_ref.shape[0]
    second = second_ref[0]
    ids = ids_ref[...]
    states = state_ref[...].astype(F32)
    starts = []
    for s in range(sequences):
        hot = (iota((tokens, length), 0) == ids[s : s + 1, :]).astype(F32).astype(BF16)
        starts.append(states[s] + t_dot(hot, table_ref[...]))
    start = jnp.concatenate(starts, 0)
    centred = start - jnp.mean(start, -1, keepdims=True)
    inverse = lax.rsqrt(jnp.mean(centred * centred, -1, keepdims=True) + EPSILON)
    if arrive is not None:
        arrive()
    projected = dot(centred.astype(BF16), weight_ref[:, channels : 3 * channels]) * inverse
    key = projected[:, :channels].astype(BF16)
    value_ref[...] = projected[:, channels:].astype(BF16)

    def mine(x):
        pairs = x.reshape(sequences * length // (2 * own_rows), 2 * own_rows, channels)
        low, high = pairs[:, :own_rows], pairs[:, own_rows:]
        return ordered(second, low, high)[0].reshape(sequences * length // 2, channels)

    start_ref[...] = mine(start)
    own = mine(centred * inverse)
    per = max(1, 8 // own_rows)
    own = own.reshape(own.shape[0] // own_rows, own_rows, channels)
    own = jnp.concatenate([own] * per, 1).reshape(-1, channels).astype(BF16)
    query = dot(own, weight_ref[:, :channels]) * (channels // heads) ** (-0.5)
    query = query.astype(BF16).astype(F32)
    gate_ref[...] = jax.nn.sigmoid(dot(own, weight_ref[:, 3 * channels :]))
    extra = (mask_ref[...].astype(F32) - 1.0) * 10000.0
    tall = query.shape[0] // sequences
    block = per * own_rows
    parts, inner = lane_parts(channels, heads)
    masks = [
        own_channels_of(block, channels // len(parts), channels // heads, h, own_rows)[None]
        for h in range(0, inner, per)
    ]
    size = len(masks) * tall
    for s in range(sequences):
        for u, part in enumerate(parts):
            rows = query[s * tall : (s + 1) * tall, part]
            rows = rows.reshape(tall // block, block, rows.shape[1])
            spread = [
                picked([rows], [mask]).reshape(tall, rows.shape[2]).astype(BF16) for mask in masks
            ]
            scores_ref[s, u * size : (u + 1) * size] = (
                dot_t(jnp.concatenate(spread, 0), key[s * length : (s + 1) * length, part]) + extra
            )

def widen(factor_ref, wide_ref, own_rows):
    width, channels = factor_ref.shape[0] // 2, factor_ref.shape[1]
    right = factor_ref[width:].astype(F32)
    repeated = jnp.broadcast_to(right[:, None, :], (width, own_rows, channels)).reshape(
        width * own_rows, channels
    )
    row = iota(repeated.shape, 0) % own_rows
    for r in range(own_rows):
        wide_ref[:, r * channels : (r + 1) * channels] = jnp.where(row == r, repeated, 0.0).astype(
            BF16
        )


def softmax_parts(scores):
    e = jnp.exp(scores - jnp.max(scores, -1, keepdims=True))
    return e.astype(BF16), 1.0 / jnp.sum(e, -1, keepdims=True)


def row_mix_kernel(
    second_ref, own_scores_ref, own_value_ref, own_gate_ref, own_start_ref,
    other_scores_ref, other_value_ref, other_gate_ref, other_start_ref,
    bias_ref, weight_ref, out_ref,
    *, heads, own_rows,
):
    sequences, expanded, length = own_scores_ref.shape
    value_ref = own_value_ref
    channels = value_ref.shape[1]
    groups = out_ref.shape[0]
    per = max(1, 8 // own_rows)
    tiles = heads // per
    block = per * own_rows
    tall = groups * block
    bias = bias_ref[...].astype(F32)
    bias = jnp.concatenate(
        [
            bias[:, t * block : (t + 1) * block].reshape(tall, length)
            for t in range(tiles)
        ],
        0,
    )
    parts, inner = lane_parts(channels, heads)
    masks = [
        own_channels_of(block, channels // len(parts), channels // heads, h, own_rows)[None]
        for h in range(0, inner, per)
    ]
    size = len(masks) * tall
    pieces = []
    sets = (
        (own_scores_ref, own_value_ref, own_gate_ref, own_start_ref),
        (other_scores_ref, other_value_ref, other_gate_ref, other_start_ref),
    )
    for (scores_ref, value_ref, gate_ref, start_ref), s in [
        (refs, s) for refs in sets for s in range(sequences)
    ]:
        weights, scale = softmax_parts(scores_ref[s] + bias)
        mixed = []
        for u, part in enumerate(parts):
            rows = slice(u * size, (u + 1) * size)
            whole = dot(weights[rows], value_ref[s * length : (s + 1) * length, part])
            whole = whole * scale[rows]
            whole = whole.reshape(len(masks), groups, block, whole.shape[1])
            mixed.append(
                picked([whole[t] for t in range(len(masks))], masks).reshape(tall, whole.shape[3])
            )
        mixed = jnp.concatenate(mixed, 1)
        gated = (gate_ref[s * tall : (s + 1) * tall] * mixed).astype(BF16)
        update = dot(gated, weight_ref[...]).reshape(groups, block, channels)
        after = start_ref[s * groups * own_rows : (s + 1) * groups * own_rows].reshape(
            groups, own_rows, channels
        )
        for h in range(per):
            after = after + update[:, h * own_rows : (h + 1) * own_rows]
        pieces.append(after)
    own, other = jnp.concatenate(pieces[:sequences], 1), jnp.concatenate(pieces[sequences:], 1)
    out_ref[...] = jnp.concatenate(ordered(second_ref[0], own, other), 1).astype(BF16)


def column_kernel(
    state_ref, weight_ref, readout_ref, factor_ref, wide_ref, out_ref, left_ref, right_ref,
    *, heads, own_rows,
):
    devices, block, channels = state_ref.shape
    size = devices * block
    sequences = size // own_rows
    to_rows = selector(size, swapped(sequences, own_rows))
    to_sequences = selector(size, swapped(own_rows, sequences))
    start = dot(to_rows, state_ref[...].reshape(size, channels))
    centred = start - jnp.mean(start, -1, keepdims=True)
    inverse = lax.rsqrt(jnp.mean(centred * centred, -1, keepdims=True) + EPSILON)
    projected = dot(centred.astype(BF16), weight_ref[...]) * inverse
    query = (projected[:, :channels] * (channels // heads) ** (-0.5)).astype(BF16).astype(F32)
    key = projected[:, channels : 2 * channels].astype(BF16)
    value = projected[:, 2 * channels : 3 * channels].astype(BF16)
    gate = jax.nn.sigmoid(projected[:, 3 * channels :])
    parts, inner = lane_parts(channels, heads)
    masks = [
        own_channels_of(1, channels // len(parts), channels // heads, h, 1) for h in range(inner)
    ]
    gated = []
    for r in range(own_rows):
        rows = slice(r * sequences, (r + 1) * sequences)
        mixed = []
        for part in parts:
            spread = [picked([query[rows, part]], [mask]).astype(BF16) for mask in masks]
            weights, scale = softmax_parts(dot_t(jnp.concatenate(spread, 0), key[rows, part]))
            whole = dot(weights, value[rows, part]) * scale
            mixed.append(
                picked(
                    [whole[h * sequences : (h + 1) * sequences] for h in range(inner)], masks
                )
            )
        gated.append((gate[rows] * jnp.concatenate(mixed, 1)).astype(BF16))
    after = start + dot(jnp.concatenate(gated, 0), readout_ref[...])
    normed = normalized(after, -1).astype(BF16)
    width = factor_ref.shape[0] // 2
    fold = max(1, 128 // sequences)
    part = width // fold
    side = jnp.concatenate(
        [normed[r * sequences : (r + 1) * sequences] for r in range(own_rows)], 1
    )
    right = dot_t(wide_ref[...], side)
    cut = part * own_rows
    right = jnp.concatenate([right[f * cut : (f + 1) * cut] for f in range(fold)], 1)
    tall = right_ref.shape[1]
    packed = jnp.concatenate(
        [right[t * tall : (t + 1) * tall] for t in range(cut // tall)], 1
    ).astype(BF16)
    for d in range(right_ref.shape[0]):
        right_ref[d] = packed
    left_ref[...] = dot_t(normed, factor_ref[:width]).astype(BF16)
    out_ref[...] = dot(to_sequences, after.astype(BF16)).astype(BF16).reshape(out_ref.shape)


def half_update(right, spread, own_rows):
    groups, tall, lanes = right.shape
    columns = spread.shape[1] * own_rows // tall
    whole = dot(right.reshape(groups * tall, lanes), spread).reshape(groups, tall, -1)
    total = whole[:, :own_rows, :columns]
    for e in range(1, tall // own_rows):
        total = total + whole[
            :, e * own_rows : (e + 1) * own_rows, e * columns : (e + 1) * columns
        ]
    return total


def spread_kernel(
    aligned_ref, right_ref, left_ref, weight_ref, out_ref, half_ref, final_ref, sem,
    *, own_rows, per,
):
    store = pltpu.make_async_copy(aligned_ref, final_ref, sem)
    store.start()
    size, width = left_ref.shape
    sequences = size // own_rows
    channels = weight_ref.shape[1] // width
    fold = max(1, 128 // sequences)
    part = width // fold
    product = dot(left_ref[...], weight_ref[...])
    for d in range(width):
        f, t, e = d // part, d % part // per, d % per
        at = (t * fold + f) * sequences
        for r in range(own_rows):
            to = (e * own_rows + r) * channels
            out_ref[at : at + sequences, to : to + channels] = product[
                r * sequences : (r + 1) * sequences, d * channels : (d + 1) * channels
            ].astype(BF16)
    half_ref[...] = half_update(right_ref[...], out_ref[...], own_rows)
    store.wait()


def pair_kernel(
    second_ref, half_ref, other_ref, spread_ref, pair_ref, weight_ref, gate_weight_ref,
    one_ref, gate_ref, out_ref,
    *, sequences,
):
    own_rows, columns, channels = pair_ref.shape
    halves = ordered(
        second_ref[0], half_ref[...], half_update(other_ref[...], spread_ref[...], own_rows)
    )
    update = jnp.concatenate(halves, 1).reshape(columns, own_rows * channels) * (1.0 / sequences)
    ones = [
        pair_ref[i].astype(F32) + update[:, i * channels : (i + 1) * channels]
        for i in range(own_rows)
    ]
    one = jnp.concatenate(ones, 0)
    one_ref[...] = one
    normed = normalized(one, -1).astype(BF16)
    gate_ref[...] = jax.nn.sigmoid(dot(normed, gate_weight_ref[...]))
    factors = dot_t(weight_ref[...], normed)
    left = jax.nn.sigmoid(factors[channels : 2 * channels]) * factors[:channels]
    right = jax.nn.sigmoid(factors[3 * channels :]) * factors[2 * channels : 3 * channels]
    both = jnp.concatenate([left.astype(BF16), right.astype(BF16)], 1)
    out_ref[...] = both.reshape(out_ref.shape)


def triangle_kernel(both_ref, out_ref, left_ref, right_ref, ordered_ref, *, own_rows):
    devices, own_channels, lanes = both_ref.shape
    columns = lanes // 2 // own_rows
    size = devices * own_channels
    tile = left_ref.shape[2]
    tiles = columns // tile
    both = both_ref[...].reshape(size, lanes).astype(F32)
    for i in range(own_rows):
        rows = slice(i * size, (i + 1) * size)
        for k in range(tiles):
            at = i * columns + k * tile
            left_ref[k, rows] = both[:, at : at + tile]
            at += own_rows * columns
            right_ref[k, rows] = both[:, at : at + tile]

    def channel_rows(c, i):
        return pl.ds(i * size + c, devices, stride=own_channels)

    for k in range(tiles):
        for c in range(own_channels):
            for i in range(own_rows):
                ordered_ref[k, pl.ds(c * columns + i, devices, stride=own_rows), :] = right_ref[
                    k, channel_rows(c, i), :
                ]
    for c in range(own_channels):
        combined = jnp.zeros((columns, columns), F32)
        for k in range(tiles):
            left = jnp.concatenate(
                [left_ref[k, channel_rows(c, i), :] for i in range(own_rows)], 0
            )
            right = ordered_ref[k, c * columns : (c + 1) * columns]
            combined = combined + dot_t(left.astype(BF16), right.astype(BF16))
        for i in range(own_rows):
            for k in range(tiles):
                right_ref[k, channel_rows(c, i), :] = combined[
                    i * devices : (i + 1) * devices, k * tile : (k + 1) * tile
                ]
    out_ref[...] = (
        jnp.concatenate(
            [
                right_ref[k, i * size : (i + 1) * size]
                for i in range(own_rows)
                for k in range(tiles)
            ],
            1,
        )
        .astype(BF16)
        .reshape(out_ref.shape)
    )


def final_kernel(back_ref, one_ref, gate_ref, weight_ref, out_ref):
    channels = weight_ref.shape[0]
    combined = back_ref[...].reshape(channels, back_ref.shape[-1]).astype(F32)
    normed = normalized(combined, 0).astype(BF16)
    update = t_dot(normed, weight_ref[...])
    out_ref[...] = (one_ref[...] + gate_ref[...] * update).astype(BF16).reshape(out_ref.shape)


def exchanged(x):
    return lax.all_to_all(x, "res", split_axis=0, concat_axis=0, tiled=True)


def shards(
    homolog_symbol_ids,
    residue_attend_mask,
    alignment_state,
    pair,
    symbol_lookup_matrix,
    pair_bias_weight,
    row_projection_weight,
    horizontal_readout_matrix,
    column_projection_weight,
    vertical_readout_matrix,
    product_factor_matrices,
    outer_output_weight,
    triangle_input_weight,
    triangle_output_weight,
):
    devices = lax.axis_size("res")
    own_sequences, length, channels = alignment_state.shape
    sequences = own_sequences * devices
    own_rows, columns, pair_channels = pair.shape
    heads = pair_bias_weight.shape[1]
    width = product_factor_matrices.shape[1] // 2
    own_channels = pair_channels // devices
    rows = own_sequences * length

    groups = [list(range(first, devices, 2)) for first in range(2)]
    half = devices // 2
    second = (lax.axis_index("res") % 2).reshape(1)

    def among_class(x):
        return lax.all_to_all(x, "res", 0, 0, axis_index_groups=groups, tiled=True)

    def from_other_core(x):
        return lax.ppermute(x, "res", [(i, i ^ 1) for i in range(devices)])

    (bias,) = kernel_call(
        bias_kernel,
        [((half, own_rows * heads, columns), BF16)],
        (pair, pair_bias_weight.T),
        "bias",
        fetched=(0, 1),
    )
    bias = among_class(bias)
    factors = product_factor_matrices.T
    parts = [
        ((own_sequences, half * own_rows * heads, length), F32),
        ((rows, channels), BF16),
        ((rows // 2 * max(1, 8 // own_rows), channels), F32),
        ((rows // 2, channels), F32),
    ]
    estimate = dict(flops=2 * rows * channels * 4 * channels, nbytes=1 << 21)
    *own, mask, table, row_weight, readout, wide = kernel_call(
        functools.partial(own_scores_kernel, heads=heads, own_rows=own_rows),
        parts
        + [
            ((1, length), jnp.int32),
            (symbol_lookup_matrix.shape, BF16),
            (row_projection_weight.shape, BF16),
            ((channels, channels), BF16),
            ((width * own_rows, own_rows * channels), BF16),
        ],
        (
            second,
            homolog_symbol_ids,
            residue_attend_mask.reshape(1, length),
            alignment_state,
            symbol_lookup_matrix,
            row_projection_weight,
            horizontal_readout_matrix,
            factors,
        ),
        "own_scores",
        scalars=1,
        fetched=(1, 3, 4, 2, 5, 6, 7),
        late=(2, 5, 6, 7),
        **estimate,
    )
    other_scores = kernel_call(
        functools.partial(other_scores_kernel, heads=heads, own_rows=own_rows),
        parts,
        (
            second,
            from_other_core(homolog_symbol_ids),
            mask,
            from_other_core(alignment_state),
            table,
            row_weight,
        ),
        "other_scores",
        scalars=1,
        **estimate,
    )
    (after_rows,) = kernel_call(
        functools.partial(row_mix_kernel, heads=heads, own_rows=own_rows),
        [((half, 2 * own_sequences * own_rows, channels), BF16)],
        (second, *own, *other_scores, bias, readout),
        "row_mix",
        scalars=1,
    )
    by_residue = among_class(after_rows)
    per = max(1, 8 // own_rows)
    aligned, left, right = kernel_call(
        functools.partial(column_kernel, heads=heads, own_rows=own_rows),
        [
            ((sequences, own_rows, channels), BF16),
            ((sequences * own_rows, width), BF16),
            ((half, per * own_rows, width * sequences // per), BF16),
        ],
        (by_residue, column_projection_weight, vertical_readout_matrix, factors, wide),
        "column",
    )
    right = among_class(right)
    other = from_other_core(right)
    inside = pl.BlockSpec(memory_space=pltpu.VMEM)
    outside = pl.BlockSpec(memory_space=pl.ANY)
    spread, update, alignment_output = pl.pallas_call(
        functools.partial(spread_kernel, own_rows=own_rows, per=per),
        out_shape=(
            jax.ShapeDtypeStruct(
                (width * sequences // per, per * own_rows * pair_channels), BF16
            ),
            jax.ShapeDtypeStruct((half, own_rows, own_rows * pair_channels), F32),
            jax.ShapeDtypeStruct(aligned.shape, BF16),
        ),
        in_specs=[inside] * 4,
        out_specs=(inside, inside, outside),
        scratch_shapes=[pltpu.SemaphoreType.DMA],
        compiler_params=pltpu.CompilerParams(vmem_limit_bytes=VMEM_BYTES),
        cost_estimate=pl.CostEstimate(
            flops=2 * own_rows * sequences * width * width * pair_channels,
            bytes_accessed=1 << 21,
            transcendentals=0,
        ),
        name="spread",
    )(aligned, right, left, outer_output_weight.reshape(width, width * pair_channels))
    pair_one, gate_out, both = kernel_call(
        functools.partial(pair_kernel, sequences=sequences),
        [
            ((own_rows * columns, pair_channels), F32),
            ((own_rows * columns, pair_channels), F32),
            ((devices, own_channels, 2 * own_rows * columns), BF16),
        ],
        (
            second,
            update,
            other,
            spread,
            pair,
            triangle_input_weight[:, : 4 * pair_channels].T,
            triangle_input_weight[:, 4 * pair_channels :],
        ),
        "pair",
        scalars=1,
    )
    both = exchanged(both)
    (combined,) = kernel_call(
        functools.partial(triangle_kernel, own_rows=own_rows),
        [((devices, own_channels, own_rows * columns), BF16)],
        (both,),
        "triangle",
        scratch=[
            pltpu.VMEM((-(-columns // 128), pair_channels * own_rows, min(columns, 128)), F32)
        ]
        * 3,
    )
    back = exchanged(combined)
    (pair_output,) = kernel_call(
        final_kernel,
        [((own_rows, columns, pair_channels), BF16)],
        (back, pair_one, gate_out, triangle_output_weight),
        "final",
    )
    return (alignment_output, pair_output)


def solution(mesh):
    placed = (
        P(("crop", "res"), None),
        P("crop"),
        P(("crop", "res"), None, None),
        P(("crop", "res"), None, None),
    ) + (P(),) * 10
    return jax.shard_map(
        shards,
        mesh=mesh,
        in_specs=placed,
        out_specs=(P("crop", "res", None), P(("crop", "res"), None, None)),
        check_vma=False,
    )
```
